512 devices in a mesh: ctx: 32 (over z, core), tp: 16 (over x, y).
Axes of the slice: x: 4, y: 4, z: 16, core: 2. Of those that a mesh axis runs over, the one named last changes fastest.
Arguments:
- hidden: bfloat16 [32768, 6144], P('ctx', 'tp'), may hold values from -6 to 6
- base_query_key_value: bfloat16 [3, 32768, 8192], P(None, 'ctx', 'tp'), may hold values from -54 to 54
- adapter_down_weight: bfloat16 [6144, 64], P('tp'), may hold values from -0.078125 to 0.078125
- adapter_up_weight: bfloat16 [3, 64, 8192], P(None, None, 'tp'), may hold values from -0.75 to 0.75
- token_log_decay: float32 [32768, 64], P('ctx', 'tp'), may hold values from -2.3 to 0, as said below
- output_norm_gain: float32 [8192], P('tp'), may hold values from 0.25 to 1.75
Outputs:
- mixed_out: bfloat16 [32768, 8192], P('ctx', 'tp')
- block_states: float32 [32, 64, 128, 128], P('ctx', 'tp')
The draws below stay inside these ranges and needn't reach their ends.
Inputs may be any that keep to these rules, and one draw needn't show every extreme that they name: `token_log_decay`: every entry is negative.
All inputs are finite; a program needn't handle non-finite values.
Results may differ from the reference program's by a relative error of at most 0.023.
Values may be sent and summed in bfloat16 or wider, within the bound.
A program may use at most 64 MiB of HBM per device.

```python
import math
import jax
import jax.numpy as jnp
from jax import lax

MODEL_WIDTH = 6144
HEAD_TOTAL = 64
HD = 128
ADAPTER_RANK = 64
TOK_DEV = 1024
SEQUENCE_TOKENS = 32768
ALL_HEAD_WIDTH = 8192
N_TP = 16


def draw_base_query_key_value(key, part):
    key = jax.random.fold_in(key, 11)
    key_raw, key_col, key_row = jax.random.split(key, 3)
    raw_values = jnp.clip(jax.random.normal(key_raw, (3, SEQUENCE_TOKENS, HEAD_TOTAL * HD), jnp.float32), -6.0, 6.0)
    col_scale = jnp.exp(jax.random.uniform(key_col, (HEAD_TOTAL * HD,), jnp.float32, math.log(0.3), math.log(3.0)))
    row_scale = jnp.exp(jax.random.uniform(key_row, (SEQUENCE_TOKENS,), jnp.float32, math.log(0.3), math.log(3.0)))
    which = jnp.arange(3)[:, None, None]
    factor = jnp.where(which == 2, row_scale[None, :, None] * col_scale[None, None, :], 1.0)
    return (raw_values * factor).astype(jnp.bfloat16)


def draw_token_log_decay(key, part):
    key = jax.random.fold_in(key, 23)
    random_keys = jax.random.split(key, 6)
    head_kind = jax.random.randint(random_keys[0], (HEAD_TOTAL,), 0, 10)
    fast_heads = head_kind < 5
    random_noise = jnp.exp(jax.random.uniform(random_keys[1], (SEQUENCE_TOKENS, HEAD_TOTAL), jnp.float32, math.log(0.5), math.log(2.0)))
    fast_rate = jnp.exp(jax.random.uniform(random_keys[2], (HEAD_TOTAL,), jnp.float32, math.log(0.75), math.log(1.33))) / 40.0
    head_decay_rate = jnp.where(fast_heads, fast_rate, 0.4 / SEQUENCE_TOKENS)
    block_factor = jnp.exp(jax.random.uniform(random_keys[3], (SEQUENCE_TOKENS // TOK_DEV, 1), jnp.float32, math.log(0.6), math.log(1.5)))
    token_decay_factor = jnp.repeat(block_factor, TOK_DEV, axis=0)
    spike_positions = jax.random.randint(random_keys[4], (3, HEAD_TOTAL), 0, SEQUENCE_TOKENS)
    spike_penalty = jax.random.uniform(random_keys[5], (3, HEAD_TOTAL), jnp.float32, 0.2, 0.5)
    token_positions = jnp.arange(SEQUENCE_TOKENS)[:, None, None]
    spike_values = jnp.sum(jnp.where(token_positions == spike_positions[None], jnp.log(1.0 - spike_penalty)[None], 0.0), axis=1)
    return -(head_decay_rate[None, :] * token_decay_factor * random_noise) + spike_values


def steps_of(key, extent, cuts, least, largest):
    gain, own = 1.0, jax.random.fold_in(key, 6)
    for dim, blocks in cuts:
        draws = jnp.exp(jax.random.uniform(jax.random.fold_in(own, dim), (blocks,), jnp.float32, least / len(cuts), largest / len(cuts)))
        gain = gain * jnp.repeat(draws, extent[dim] // blocks).reshape([-1 if axis == dim else 1 for axis in range(len(extent))])
    return gain


def noise(own_key, dims, width, reach, cuts=(), held_as=jnp.bfloat16):
    factor_of = steps_of(own_key, dims, cuts, -0.22, 0.18) if cuts else 1.0
    array = jax.random.normal(own_key, dims, jnp.float32) * width * factor_of
    return jnp.minimum(jnp.maximum(array, -reach), reach).astype(held_as)


def setup_inputs(seed: int = 0) -> dict:
    arg_keys = jax.random.split(jax.random.key(seed), 7)
    return {
        "hidden": noise(arg_keys[0], (SEQUENCE_TOKENS, MODEL_WIDTH), 1.0, 6.0, ((0, 32), (1, 16))),
        "base_query_key_value": draw_base_query_key_value(jax.random.fold_in(arg_keys[6], 71), 0),
        "adapter_down_weight": noise(arg_keys[2], (MODEL_WIDTH, ADAPTER_RANK), MODEL_WIDTH ** -0.5, 0.078125, ((0, 16),)),
        "adapter_up_weight": noise(arg_keys[3], (3, ADAPTER_RANK, ALL_HEAD_WIDTH), ADAPTER_RANK ** -0.5, 0.75, ((2, 16),)),
        "token_log_decay": draw_token_log_decay(jax.random.fold_in(arg_keys[6], 71), 0),
        "output_norm_gain": jnp.clip(1.0 + 0.15 * jax.random.normal(arg_keys[5], (ALL_HEAD_WIDTH,), jnp.float32), 0.25, 1.75),
    }


def reference(hidden, base_query_key_value, adapter_down_weight, adapter_up_weight, token_log_decay, output_norm_gain):
    block_count = SEQUENCE_TOKENS // TOK_DEV
    group_width = MODEL_WIDTH // N_TP
    head_gain = output_norm_gain.reshape(HEAD_TOTAL, HD)
    causal = jnp.arange(TOK_DEV)[:, None] >= jnp.arange(TOK_DEV)[None, :]
    grouped_down_weight = adapter_down_weight.astype(jnp.float32).reshape(N_TP, group_width, ADAPTER_RANK)

    def one_block(state, block_index):
        first_row = (block_index * TOK_DEV).astype(jnp.int32)
        token_rows = lax.dynamic_slice_in_dim(hidden, first_row, TOK_DEV, 0)
        grouped_token_rows = token_rows.astype(jnp.float32).reshape(TOK_DEV, N_TP, group_width)
        low_rank_pieces = jnp.einsum('vsx,sxj->svj', grouped_token_rows, grouped_down_weight).astype(jnp.bfloat16).astype(jnp.float32)
        adapter_row_values = lax.optimization_barrier(jnp.sum(low_rank_pieces, axis=0))
        adapter_hidden = adapter_row_values.astype(jnp.bfloat16)
        base_token_rows = lax.dynamic_slice_in_dim(base_query_key_value, first_row, TOK_DEV, 1)
        projected_rows = base_token_rows.astype(jnp.float32) + jnp.einsum('uz,ozh->ouh', adapter_hidden.astype(jnp.float32), adapter_up_weight.astype(jnp.float32))
        query = jax.nn.silu(projected_rows[0]).astype(jnp.bfloat16).astype(jnp.float32).reshape(TOK_DEV, HEAD_TOTAL, HD)
        key_rows = jax.nn.silu(projected_rows[1]).astype(jnp.bfloat16).astype(jnp.float32).reshape(TOK_DEV, HEAD_TOTAL, HD)
        value = projected_rows[2].astype(jnp.bfloat16).astype(jnp.float32).reshape(TOK_DEV, HEAD_TOTAL, HD)
        gate_rows = lax.dynamic_slice_in_dim(token_log_decay, first_row, TOK_DEV, 0)
        cumulative = jnp.cumsum(gate_rows, axis=0)
        scores = jnp.einsum('thd,shd->hts', query, key_rows)
        spread = cumulative.T[:, :, None] - cumulative.T[:, None, :]
        decayed = jnp.exp(jnp.where(causal[None], spread, 0.0))
        weights = jnp.where(causal[None], decayed * scores, 0.0).astype(jnp.bfloat16).astype(jnp.float32)
        inside = jnp.einsum('hts,shd->thd', weights, value)
        last_sum = cumulative[-1]
        key_scaled = (key_rows * jnp.exp(last_sum[None, :] - cumulative)[:, :, None]).astype(jnp.bfloat16).astype(jnp.float32)
        local_state = jnp.einsum('shd,she->hde', key_scaled, value)
        carried = state.astype(jnp.bfloat16).astype(jnp.float32)
        preceding_blocks = jnp.einsum('thd,hde->the', query, carried) * jnp.exp(cumulative)[:, :, None]
        attended = inside + preceding_blocks
        mean_square = lax.optimization_barrier(jnp.mean(attended * attended, axis=-1, keepdims=True))
        normed = attended * lax.rsqrt(mean_square + 1e-06) * head_gain[None]
        mixed = normed.reshape(TOK_DEV, HEAD_TOTAL * HD).astype(jnp.bfloat16)
        new_state = jnp.exp(last_sum)[:, None, None] * state + local_state
        return (new_state, (mixed, new_state))
    final_state, (mixed_rows, states) = lax.scan(one_block, jnp.zeros((HEAD_TOTAL, HD, HD), jnp.float32), jnp.arange(block_count, dtype=jnp.int32))
    return (mixed_rows.reshape(SEQUENCE_TOKENS, HEAD_TOTAL * HD), states)
```

```python
import jax
import jax.numpy as jnp
from jax import lax
from jax.experimental import pallas as pl
from jax.experimental.pallas import tpu as pltpu
from jax.sharding import PartitionSpec as P

HD = 128
HEADS = 4
TOK = 1024
HALF = 512
RANK = 64
GROUP = 384
WIDTH = HEADS * HD
PAIR = 2 * HD
BLK = 256
NX, NY, NZ = 4, 4, 16
NTP = NX * NY
LORA_PIECE = HALF // NTP
STATE_PIECE = PAIR // NZ
MESH = pl.DeviceIdType.MESH
F32, BF16 = jnp.float32, jnp.bfloat16


def ring(offset, size):
    return min(offset, size - offset)


XY = sorted(range(1, NTP), key=lambda r: -(ring(r // NY, NX) + ring(r % NY, NY)))
ZZ = sorted(range(1, NZ), key=lambda r: -ring(r, NZ))


def silu(v):
    half = 0.5 * v
    return half + half * jnp.tanh(half)


def kernel(
    hid_hbm, base_hbm, dwn_hbm, up_hbm, dec_hbm, gain_hbm,
    out_hbm, st_hbm,
    hid, base, dpad, upad, dec, gain,
    part, rsum, lora,
    cum, wgt, ccol, dl_own, dl_peer, dl_chip,
    q_ref, qs_ref, kt_ref, v_ref, inside, out_v,
    loc, loc_send, loc_recv, tot, p1, pre, c2, carried, st_v,
    in_sem, out_sem, st_sem,
    rs_s, rs_r, ag_s, ag_r, zs_s, zs_r, zg_s, zg_r, dz_s, dz_r, core_s, core_r,
):
    ctx, tp = lax.axis_index("ctx"), lax.axis_index("tp")
    z, c = ctx // 2, ctx % 2
    x, y = tp // NY, tp % NY
    peer = {"ctx": z * 2 + (1 - c)}

    def plane(r):
        return {"tp": lax.rem(x + r // NY, NX) * NY + lax.rem(y + r % NY, NY)}

    def along(r):
        return {"ctx": lax.rem(z + r, NZ) * 2 + c}

    barrier = pltpu.get_barrier_semaphore()
    for r in ZZ:
        pl.semaphore_signal(barrier, inc=1, device_id=along(r), device_id_type=MESH)
    for r in XY:
        pl.semaphore_signal(barrier, inc=1, device_id=plane(r), device_id_type=MESH)
    pl.semaphore_signal(barrier, inc=1, device_id=peer, device_id_type=MESH)

    loads = [
        pltpu.make_async_copy(dwn_hbm, dpad.at[pl.ds(RANK, RANK)], in_sem.at[0]),
        pltpu.make_async_copy(hid_hbm, hid, in_sem.at[1]),
        pltpu.make_async_copy(dec_hbm, dec, in_sem.at[2]),
        pltpu.make_async_copy(up_hbm, upad.at[:, pl.ds(RANK, RANK)], in_sem.at[3]),
        pltpu.make_async_copy(base_hbm, base, in_sem.at[4]),
        pltpu.make_async_copy(gain_hbm, gain, in_sem.at[5]),
    ]
    for load in loads:
        load.start()

    zeros = jnp.zeros((RANK, GROUP), BF16)
    dpad[pl.ds(0, RANK), :] = zeros
    dpad[pl.ds(2 * RANK, RANK), :] = zeros
    zeros = jnp.zeros((RANK, WIDTH), BF16)
    for i in range(3):
        upad[i, pl.ds(0, RANK), :] = zeros
        upad[i, pl.ds(2 * RANK, RANK), :] = zeros

    loads[0].wait()
    loads[1].wait()
    trans_b = (((1,), (1,)), ((), ()))
    for i in range(2):
        rows = pl.ds(i * BLK, BLK)
        mine = lax.dot_general(
            hid[rows, :], dpad[pl.ds(RANK, 2 * RANK), :], trans_b, preferred_element_type=F32
        ) + lax.dot_general(
            hid[pl.ds(HALF + i * BLK, BLK), :], dpad[pl.ds(0, 2 * RANK), :], trans_b,
            preferred_element_type=F32,
        )
        part[rows, :] = mine.astype(BF16)

    pl.semaphore_wait(barrier, NTP - 1 + NZ - 1 + 1)

    def rs(r):
        to = plane(r)
        return pltpu.make_async_remote_copy(
            part.at[pl.ds(pl.multiple_of(to["tp"] * LORA_PIECE, LORA_PIECE), LORA_PIECE)],
            rsum.at[r], rs_s.at[r], rs_r.at[r], device_id=to, device_id_type=MESH,
        )

    for r in XY:
        rs(r).start()

    loads[2].wait()
    run = jnp.concatenate([dec[...], jnp.zeros((8 - HEADS, TOK), F32)], axis=0)
    lane = lax.broadcasted_iota(jnp.int32, (8, TOK), 1)
    step = 1
    while step < TOK:
        run = run + jnp.where(lane >= step, pltpu.roll(run, step, 1), 0.0)
        step *= 2
    last = run[:, TOK - 1 :]
    cum[...] = run
    wgt[...] = jnp.exp(last - run)
    dl_own[...] = jnp.broadcast_to(last, (8, HD))
    swap_decay = pltpu.make_async_remote_copy(
        dl_own, dl_peer, core_s.at[0], core_r.at[0], device_id=peer, device_id_type=MESH
    )
    swap_decay.start()

    def ccol_of(h, carry):
        ccol[h] = jnp.broadcast_to(cum[pl.ds(h, 1), :], (HD, TOK)).T
        return carry

    lax.fori_loop(0, HEADS, ccol_of, 0)

    swap_decay.wait()
    dl_chip[z] = dl_own[...] + dl_peer[...]

    def dz(r):
        return pltpu.make_async_remote_copy(
            dl_chip.at[z], dl_chip.at[z], dz_s.at[r], dz_r.at[r],
            device_id=along(r), device_id_type=MESH,
        )

    for r in ZZ:
        dz(r).start()

    mine_at = pl.ds(pl.multiple_of(tp * LORA_PIECE, LORA_PIECE), LORA_PIECE)
    for r in XY:
        rs(r).wait_recv()
    total = part[mine_at, :].astype(F32)
    for r in range(1, NTP):
        total = total + rsum[r].astype(F32)
    lora[mine_at, :] = total.astype(BF16)

    def ag(r):
        return pltpu.make_async_remote_copy(
            lora.at[mine_at], lora.at[mine_at], ag_s.at[r], ag_r.at[r],
            device_id=plane(r), device_id_type=MESH,
        )

    for r in XY:
        ag(r).start()
    for r in XY:
        rs(r).wait_send()
    for r in ZZ:
        dz(r).wait()
    loads[3].wait()
    loads[4].wait()
    loads[5].wait()
    for r in XY:
        ag(r).wait_recv()

    def projected(i, a, row, lanes):
        return base[i, pl.ds(a * HALF + row, BLK), lanes].astype(F32) + jnp.dot(
            lora[pl.ds(row, BLK), :],
            upad[i, pl.ds(RANK - RANK * a, 2 * RANK), lanes],
            preferred_element_type=F32,
        )

    def keys_values(pair):
        lanes = pl.ds(pl.multiple_of(pair * PAIR, PAIR), PAIR)
        for a in range(2):
            for row in range(0, HALF, BLK):
                rows = pl.ds(a * HALF + row, BLK)
                k = silu(projected(1, a, row, lanes)).astype(BF16)
                kt_ref[lanes, rows] = k.T
                v_ref[rows, lanes] = projected(2, a, row, lanes).astype(BF16)
        for e in range(2):
            h = pair * 2 + e
            at = pl.ds(pl.multiple_of(h * HD, HD), HD)
            scaled = (kt_ref[at, :].astype(F32) * wgt[pl.ds(h, 1), :]).astype(BF16)
            loc[at, :] = jnp.dot(scaled, v_ref[:, at], preferred_element_type=F32)

    ours = pl.ds(pl.multiple_of(c * PAIR, PAIR), PAIR)
    theirs = pl.ds(pl.multiple_of((1 - c) * PAIR, PAIR), PAIR)
    even = c == 0

    keys_values(1 - c)
    loc_send[...] = loc[theirs, :].astype(BF16)
    swap_local = pltpu.make_async_remote_copy(
        loc_send, loc_recv, core_s.at[1], core_r.at[1], device_id=peer, device_id_type=MESH
    )
    swap_local.start()
    keys_values(c)
    swap_local.wait()

    def per_row(ref, e):
        return jnp.exp(ref[pl.ds(c * 2 + e, 1), :])

    for e in range(2):
        rows = pl.ds(e * HD, HD)
        own = loc[pl.ds(pl.multiple_of(c * PAIR + e * HD, HD), HD), :]
        other = loc_recv[rows, :].astype(F32)
        odd_decay = jnp.where(even, per_row(dl_peer, e), per_row(dl_own, e))
        tot[rows, :] = (
            jnp.where(even, own, other) * odd_decay + jnp.where(even, other, own)
        ).astype(BF16)

    def zs(r):
        to = along(r)
        there = lax.rem(z + r, NZ)
        return pltpu.make_async_remote_copy(
            tot.at[pl.ds(pl.multiple_of(there * STATE_PIECE, STATE_PIECE), STATE_PIECE)],
            p1.at[z], zs_s.at[r], zs_r.at[r], device_id=to, device_id_type=MESH,
        )

    for r in ZZ:
        zs(r).start()
    piece_at = pl.ds(pl.multiple_of(z * STATE_PIECE, STATE_PIECE), STATE_PIECE)
    p1[z] = tot[piece_at, :]

    def queries(i, carry):
        for a in range(2):
            row = pl.multiple_of(i * BLK, BLK)
            rows = pl.ds(a * HALF + row, BLK)
            q = silu(projected(0, a, row, pl.ds(0, WIDTH))).astype(BF16)
            q_ref[rows, :] = q
            for h in range(HEADS):
                grow = jnp.exp(ccol[h, rows, :])
                qs_ref[rows, h * HD : (h + 1) * HD] = (
                    q[:, h * HD : (h + 1) * HD].astype(F32) * grow
                ).astype(BF16)
        return carry

    tri = lax.broadcasted_iota(jnp.int32, (BLK, BLK), 0) >= lax.broadcasted_iota(
        jnp.int32, (BLK, BLK), 1
    )

    def attend(h, carry):
        at = pl.ds(pl.multiple_of(h * HD, HD), HD)
        for b in range(TOK // BLK):
            rows = pl.ds(b * BLK, BLK)
            q = q_ref[rows, at]
            col = ccol[h, rows, :]
            col = jnp.concatenate([col, col], axis=1)
            acc = jnp.zeros((BLK, HD), F32)
            for s in range(b + 1):
                cols = pl.ds(s * BLK, BLK)
                spread = col - cum[pl.ds(h, 1), cols]
                if s == b:
                    spread = jnp.where(tri, spread, -1e30)
                score = jnp.dot(q, kt_ref[at, cols], preferred_element_type=F32)
                weight = (jnp.exp(spread) * score).astype(BF16)
                acc = acc + jnp.dot(weight, v_ref[cols, at], preferred_element_type=F32)
            inside[rows, at] = acc
        return carry

    lax.fori_loop(0, HALF // BLK, queries, 0)
    lax.fori_loop(0, HEADS // 2, attend, 0)

    for r in ZZ:
        zs(r).wait_recv()
    head = c * 2 + z // (NZ // 2)
    state = jnp.zeros((STATE_PIECE, HD), F32)
    for k in range(NZ):
        pre[k] = state.astype(BF16)
        state = jnp.exp(dl_chip[k, pl.ds(head, 1), :]) * state + p1[k].astype(F32)

    def zg(r):
        there = lax.rem(z + r, NZ)
        return pltpu.make_async_remote_copy(
            pre.at[there], c2.at[piece_at], zg_s.at[r], zg_r.at[r],
            device_id=along(r), device_id_type=MESH,
        )

    for r in ZZ:
        zg(r).start()
    c2[piece_at, :] = pre[z]
    lax.fori_loop(HEADS // 2, HEADS, attend, 0)
    for r in XY:
        ag(r).wait_send()
    for r in ZZ:
        zs(r).wait_send()
    for r in ZZ:
        zg(r).wait_recv()

    for e in range(2):
        rows = pl.ds(e * HD, HD)
        at = pl.ds(pl.multiple_of(c * PAIR + e * HD, HD), HD)
        own = loc[at, :]
        before = c2[rows, :].astype(F32)
        even_decay = jnp.where(even, per_row(dl_own, e), per_row(dl_peer, e))
        after = even_decay * before + jnp.where(even, own, loc_recv[rows, :].astype(F32))
        loc_send[rows, :] = jnp.where(even, after, before).astype(BF16)
        here = jnp.where(even, before, after)
        carried[at, :] = here.astype(BF16)
        st_v[at, :] = per_row(dl_own, e) * here + own
    swap_carried = pltpu.make_async_remote_copy(
        loc_send, carried.at[ours], core_s.at[2], core_r.at[2],
        device_id=peer, device_id_type=MESH,
    )
    swap_carried.start()

    def write(pair, b, slot):
        rows = pl.ds(b * BLK, BLK)
        lanes = pl.ds(pl.multiple_of(pair * PAIR, PAIR), PAIR)
        return pltpu.make_async_copy(
            out_v.at[rows, lanes], out_hbm.at[rows, lanes], out_sem.at[slot]
        )

    def finish(pair, slot):
        for b in range(TOK // BLK):
            rows = pl.ds(b * BLK, BLK)
            for e in range(2):
                at = pl.ds(pl.multiple_of(pair * PAIR + e * HD, HD), HD)
                att = inside[rows, at] + jnp.dot(
                    qs_ref[rows, at], carried[at, :], preferred_element_type=F32
                )
                square = jnp.mean(att * att, axis=-1, keepdims=True)
                out_v[rows, at] = (
                    att * lax.rsqrt(square + 1e-6) * gain[pl.ds(pair * 2 + e, 1), :]
                ).astype(BF16)
            write(pair, b, slot * 4 + b).start()

    finish(c, 0)
    swap_carried.wait()
    for e in range(2):
        at = pl.ds(pl.multiple_of((1 - c) * PAIR + e * HD, HD), HD)
        decay = jnp.exp(dl_own[pl.ds((1 - c) * 2 + e, 1), :])
        st_v[at, :] = decay * carried[at, :].astype(F32) + loc[at, :]
    store_state = pltpu.make_async_copy(st_v, st_hbm, st_sem)
    store_state.start()
    finish(1 - c, 1)
    for r in ZZ:
        zg(r).wait_send()
    for b in range(TOK // BLK):
        write(c, b, b).wait()
        write(1 - c, b, 4 + b).wait()
    store_state.wait()


def local(hidden, base, down, up, decay, gain):
    anyspace = pl.BlockSpec(memory_space=pl.ANY)
    dma = pltpu.SemaphoreType.DMA
    scratch = [
        pltpu.VMEM((TOK, GROUP), BF16),
        pltpu.VMEM((3, TOK, WIDTH), BF16),
        pltpu.VMEM((3 * RANK, GROUP), BF16),
        pltpu.VMEM((3, 3 * RANK, WIDTH), BF16),
        pltpu.VMEM((HEADS, TOK), F32),
        pltpu.VMEM((HEADS, HD), F32),
        pltpu.VMEM((HALF, 2 * RANK), BF16),
        pltpu.VMEM((NTP, LORA_PIECE, 2 * RANK), BF16),
        pltpu.VMEM((HALF, 2 * RANK), BF16),
        pltpu.VMEM((8, TOK), F32),
        pltpu.VMEM((8, TOK), F32),
        pltpu.VMEM((HEADS, TOK, HD), F32),
        pltpu.VMEM((8, HD), F32),
        pltpu.VMEM((8, HD), F32),
        pltpu.VMEM((NZ, 8, HD), F32),
        pltpu.VMEM((TOK, WIDTH), BF16),
        pltpu.VMEM((TOK, WIDTH), BF16),
        pltpu.VMEM((WIDTH, TOK), BF16),
        pltpu.VMEM((TOK, WIDTH), BF16),
        pltpu.VMEM((TOK, WIDTH), F32),
        pltpu.VMEM((TOK, WIDTH), BF16),
        pltpu.VMEM((WIDTH, HD), F32),
        pltpu.VMEM((PAIR, HD), BF16),
        pltpu.VMEM((PAIR, HD), BF16),
        pltpu.VMEM((PAIR, HD), BF16),
        pltpu.VMEM((NZ, STATE_PIECE, HD), BF16),
        pltpu.VMEM((NZ, STATE_PIECE, HD), BF16),
        pltpu.VMEM((PAIR, HD), BF16),
        pltpu.VMEM((WIDTH, HD), BF16),
        pltpu.VMEM((WIDTH, HD), F32),
        dma((6,)), dma((8,)), dma,
        dma((NTP,)), dma((NTP,)), dma((NTP,)), dma((NTP,)),
        dma((NZ,)), dma((NZ,)), dma((NZ,)), dma((NZ,)), dma((NZ,)), dma((NZ,)),
        dma((3,)), dma((3,)),
    ]
    mixed, states = pl.pallas_call(
        kernel,
        out_shape=(
            jax.ShapeDtypeStruct((TOK, WIDTH), BF16),
            jax.ShapeDtypeStruct((WIDTH, HD), F32),
        ),
        in_specs=[anyspace] * 6,
        out_specs=(anyspace, anyspace),
        scratch_shapes=scratch,
        compiler_params=pltpu.CompilerParams(
            collective_id=0, has_side_effects=True, vmem_limit_bytes=48 * 1024 * 1024
        ),
        cost_estimate=pl.CostEstimate(
            flops=3_000_000_000, bytes_accessed=6_000_000, transcendentals=6_000_000
        ),
    )(hidden, base, down.T, up, decay.T, gain.reshape(HEADS, HD))
    return mixed, states.reshape(1, HEADS, HD, HD)


def solution(mesh):
    in_specs = (
        P("ctx", "tp"),
        P(None, "ctx", "tp"),
        P("tp", None),
        P(None, None, "tp"),
        P("ctx", "tp"),
        P("tp"),
    )
    out_specs = (P("ctx", "tp"), P("ctx", "tp", None, None))
    return jax.shard_map(local, mesh=mesh, in_specs=in_specs, out_specs=out_specs, check_vma=False)
```

```python
import jax
import jax.numpy as jnp
from jax import lax
from jax.experimental import pallas as pl
from jax.experimental.pallas import tpu as pltpu
from jax.sharding import PartitionSpec as P

HD = 128
HEADS = 4
TOK = 1024
HALF = 512
RANK = 64
GROUP = 384
WIDTH = HEADS * HD
PAIR = 2 * HD
BLK = 256
NX, NY, NZ = 4, 4, 16
NTP = NX * NY
LORA_PIECE = HALF // NTP
CHUNK = HALF // NX
HZ = NZ // 2
STATE_PIECE = PAIR // HZ
MESH = pl.DeviceIdType.MESH
F32, BF16 = jnp.float32, jnp.bfloat16


def ring(offset, size):
    return min(offset, size - offset)


XY = sorted(range(1, NTP), key=lambda r: -(ring(r // NY, NX) + ring(r % NY, NY)))
ZH = [4, 3, 5, 2, 6, 1, 7]


def order(z):
    return jnp.where(z < HZ, z, jnp.where(z >= 12, 23 - z, z + 4))


ORDER = [z if z < HZ else (23 - z if z >= 12 else z + 4) for z in range(NZ)]


def silu(v):
    half = 0.5 * v
    return half + half * jnp.tanh(half)


def kernel(
    hid_hbm, base_hbm, dwn_hbm, up_hbm, dec_hbm, gain_hbm,
    out_hbm, st_hbm,
    hid, base, dpad, upad, dec, gain,
    part, rsum, lora,
    cum, wgt, ccol, dl_own, dl_peer, dl_chip,
    q_ref, qs_ref, kt_ref, v_ref, inside, out_v,
    loc, loc_send, loc_recv, tot, p1, pre, c2, carried, st_v,
    in_sem, out_sem, st_sem,
    rs_s, rs_r, ag_s, ag_r, zs_s, zs_r, zg_s, zg_r, dz_s, dz_r, core_s, core_r, near_sem, far_sem,
):
    ctx, tp = lax.axis_index("ctx"), lax.axis_index("tp")
    z, c = ctx // 2, ctx % 2
    x, y = tp // NY, tp % NY
    peer = {"ctx": z * 2 + (1 - c)}

    def plane(r):
        return {"tp": lax.rem(x + r // NY, NX) * NY + lax.rem(y + r % NY, NY)}

    zh = z % HZ
    base_z = z - zh
    lower = z < HZ

    def chip(other):
        return {"ctx": other * 2 + c}

    def along(r):
        return base_z + lax.rem(zh + r, HZ)

    place = order(z)
    barrier = pltpu.get_barrier_semaphore()
    for r in XY:
        pl.semaphore_signal(barrier, inc=1, device_id=plane(r), device_id_type=MESH)
    pl.semaphore_signal(barrier, inc=1, device_id=peer, device_id_type=MESH)
    for k in range(NZ):
        @pl.when(place < ORDER[k])
        def _(k=k):
            pl.semaphore_signal(barrier, inc=1, device_id=chip(k), device_id_type=MESH)

    loads = [
        pltpu.make_async_copy(dwn_hbm, dpad.at[pl.ds(RANK, RANK)], in_sem.at[0]),
        pltpu.make_async_copy(hid_hbm, hid, in_sem.at[1]),
        pltpu.make_async_copy(dec_hbm, dec, in_sem.at[2]),
        pltpu.make_async_copy(up_hbm, upad.at[:, pl.ds(RANK, RANK)], in_sem.at[3]),
        pltpu.make_async_copy(base_hbm, base, in_sem.at[4]),
        pltpu.make_async_copy(gain_hbm, gain, in_sem.at[5]),
    ]
    for load in loads:
        load.start()

    zeros = jnp.zeros((RANK, GROUP), BF16)
    dpad[pl.ds(0, RANK), :] = zeros
    dpad[pl.ds(2 * RANK, RANK), :] = zeros
    zeros = jnp.zeros((RANK, WIDTH), BF16)
    for i in range(3):
        upad[i, pl.ds(0, RANK), :] = zeros
        upad[i, pl.ds(2 * RANK, RANK), :] = zeros

    loads[0].wait()
    loads[1].wait()
    trans_b = (((1,), (1,)), ((), ()))
    for i in range(2):
        rows = pl.ds(i * BLK, BLK)
        mine = lax.dot_general(
            hid[rows, :], dpad[pl.ds(RANK, 2 * RANK), :], trans_b, preferred_element_type=F32
        ) + lax.dot_general(
            hid[pl.ds(HALF + i * BLK, BLK), :], dpad[pl.ds(0, 2 * RANK), :], trans_b,
            preferred_element_type=F32,
        )
        part[rows, :] = mine.astype(BF16)

    pl.semaphore_wait(barrier, NTP - 1 + 1 + place)

    def rs(r):
        to = plane(r)
        return pltpu.make_async_remote_copy(
            part.at[pl.ds(pl.multiple_of(to["tp"] * LORA_PIECE, LORA_PIECE), LORA_PIECE)],
            rsum.at[r], rs_s.at[r], rs_r.at[r], device_id=to, device_id_type=MESH,
        )

    for r in XY:
        rs(r).start()

    for k in range(NZ):
        same = lower if k < HZ else jnp.logical_not(lower)

        @pl.when(jnp.logical_and(place > ORDER[k], same))
        def _(k=k):
            pl.semaphore_signal(near_sem, inc=1, device_id=chip(k), device_id_type=MESH)

        @pl.when(jnp.logical_and(place > ORDER[k], jnp.logical_not(same)))
        def _(k=k):
            pl.semaphore_signal(far_sem, inc=1, device_id=chip(k), device_id_type=MESH)

    loads[2].wait()
    run = jnp.concatenate([dec[...], jnp.zeros((8 - HEADS, TOK), F32)], axis=0)
    lane = lax.broadcasted_iota(jnp.int32, (8, TOK), 1)
    step = 1
    while step < TOK:
        run = run + jnp.where(lane >= step, pltpu.roll(run, step, 1), 0.0)
        step *= 2
    last = run[:, TOK - 1 :]
    cum[...] = run
    wgt[...] = jnp.exp(last - run)
    dl_own[...] = jnp.broadcast_to(last, (8, HD))
    swap_decay = pltpu.make_async_remote_copy(
        dl_own, dl_peer, core_s.at[0], core_r.at[0], device_id=peer, device_id_type=MESH
    )
    swap_decay.start()

    def ccol_of(h, carry):
        ccol[h] = jnp.broadcast_to(cum[pl.ds(h, 1), :], (HD, TOK)).T
        return carry

    lax.fori_loop(0, HEADS, ccol_of, 0)

    swap_decay.wait()
    dl_chip[z] = dl_own[...] + dl_peer[...]

    def dz(other, slot):
        return pltpu.make_async_remote_copy(
            dl_chip.at[z], dl_chip.at[z], dz_s.at[slot], dz_r.at[z],
            device_id=chip(other), device_id_type=MESH,
        )

    def dz_from(k):
        return pltpu.make_async_remote_copy(
            dl_chip.at[k], dl_chip.at[k], dz_s.at[0], dz_r.at[k],
            device_id=peer, device_id_type=MESH,
        )

    mine_at = pl.ds(pl.multiple_of(tp * LORA_PIECE, LORA_PIECE), LORA_PIECE)
    for r in XY:
        rs(r).wait_recv()
    total = part[mine_at, :].astype(F32)
    for r in range(1, NTP):
        total = total + rsum[r].astype(F32)
    lora[mine_at, :] = total.astype(BF16)

    def ag(r):
        return pltpu.make_async_remote_copy(
            lora.at[mine_at], lora.at[mine_at], ag_s.at[r], ag_r.at[r],
            device_id=plane(r), device_id_type=MESH,
        )

    for r in XY:
        ag(r).start()
    for r in XY:
        rs(r).wait_send()
    later = jnp.where(lower, HZ, NZ) - 1 - place

    @pl.when(later > 0)
    def _():
        pl.semaphore_wait(near_sem, later)

    for r in ZH:
        dz(along(r), r).start()
    loads[3].wait()
    loads[4].wait()
    loads[5].wait()

    def projected(i, a, row, size, lanes):
        return base[i, pl.ds(a * HALF + row, size), lanes].astype(F32) + jnp.dot(
            lora[pl.ds(row, size), :],
            upad[i, pl.ds(RANK - RANK * a, 2 * RANK), lanes],
            preferred_element_type=F32,
        )

    for n, shift in enumerate((0, 1, 3, 2)):
        for ry in range(NY):
            if shift or ry:
                ag(shift * NY + ry).wait_recv()
        row = pl.multiple_of(lax.rem(x + NX - shift, NX) * CHUNK, CHUNK)
        scaled = []
        for a in range(2):
            at = pl.ds(pl.multiple_of(a * HALF + row, CHUNK), CHUNK)
            k = silu(projected(1, a, row, CHUNK, slice(None))).astype(BF16).T
            kt_ref[:, at] = k
            v_ref[at, :] = projected(2, a, row, CHUNK, slice(None)).astype(BF16)
            scaled.append(
                [
                    (k[h * HD : (h + 1) * HD].astype(F32) * wgt[h : h + 1, at]).astype(BF16)
                    for h in range(HEADS)
                ]
            )
        for h in range(HEADS):
            lanes = slice(h * HD, (h + 1) * HD)
            part_sum = sum(
                jnp.dot(
                    scaled[a][h],
                    v_ref[pl.ds(pl.multiple_of(a * HALF + row, CHUNK), CHUNK), lanes],
                    preferred_element_type=F32,
                )
                for a in range(2)
            )
            if n == 0:
                loc[lanes, :] = part_sum
            else:
                loc[lanes, :] += part_sum

    ours = pl.ds(pl.multiple_of(c * PAIR, PAIR), PAIR)
    theirs = pl.ds(pl.multiple_of((1 - c) * PAIR, PAIR), PAIR)
    even = c == 0

    loc_send[...] = loc[theirs, :].astype(BF16)
    swap_local = pltpu.make_async_remote_copy(
        loc_send, loc_recv, core_s.at[1], core_r.at[1], device_id=peer, device_id_type=MESH
    )
    swap_local.start()
    for r in ZH:
        dz(along(r), r).wait_send()
    swap_local.wait()

    def per_row(ref, e):
        return jnp.exp(ref[pl.ds(c * 2 + e, 1), :])

    for e in range(2):
        rows = pl.ds(e * HD, HD)
        own = loc[pl.ds(pl.multiple_of(c * PAIR + e * HD, HD), HD), :]
        other = loc_recv[rows, :].astype(F32)
        odd_decay = jnp.where(even, per_row(dl_peer, e), per_row(dl_own, e))
        tot[rows, :] = (
            jnp.where(even, own, other) * odd_decay + jnp.where(even, other, own)
        ).astype(BF16)

    def zs(other, slot):
        rows = pl.ds(pl.multiple_of((other % HZ) * STATE_PIECE, STATE_PIECE), STATE_PIECE)
        return pltpu.make_async_remote_copy(
            tot.at[rows], p1.at[z], zs_s.at[slot], zs_r.at[z],
            device_id=chip(other), device_id_type=MESH,
        )

    def zs_from(k):
        return pltpu.make_async_remote_copy(
            tot.at[pl.ds(0, STATE_PIECE)], p1.at[k], zs_s.at[0], zs_r.at[k],
            device_id=peer, device_id_type=MESH,
        )

    @pl.when(zh < HZ - 1)
    def _():
        for r in ZH:
            zs(along(r), r).start()

    @pl.when(lower)
    def _():
        pl.semaphore_wait(far_sem, HZ)
        for r in range(HZ):
            dz(HZ + lax.rem(z + r, HZ), HZ + r).start()
            zs(HZ + lax.rem(z + r, HZ), HZ + r).start()

    piece_at = pl.ds(pl.multiple_of(zh * STATE_PIECE, STATE_PIECE), STATE_PIECE)
    p1[z] = tot[piece_at, :]

    def queries(i, carry):
        for a in range(2):
            row = pl.multiple_of(i * BLK, BLK)
            rows = pl.ds(a * HALF + row, BLK)
            q = silu(projected(0, a, row, BLK, slice(None))).astype(BF16)
            q_ref[rows, :] = q
            for h in range(HEADS):
                grow = jnp.exp(ccol[h, rows, :])
                qs_ref[rows, h * HD : (h + 1) * HD] = (
                    q[:, h * HD : (h + 1) * HD].astype(F32) * grow
                ).astype(BF16)
        return carry

    tri = lax.broadcasted_iota(jnp.int32, (BLK, BLK), 0) >= lax.broadcasted_iota(
        jnp.int32, (BLK, BLK), 1
    )

    def attend(h, carry):
        at = pl.ds(pl.multiple_of(h * HD, HD), HD)
        for b in range(TOK // BLK):
            rows = pl.ds(b * BLK, BLK)
            q = q_ref[rows, at]
            col = ccol[h, rows, :]
            col = jnp.concatenate([col, col], axis=1)
            acc = jnp.zeros((BLK, HD), F32)
            for s in range(b + 1):
                cols = pl.ds(s * BLK, BLK)
                spread = col - cum[pl.ds(h, 1), cols]
                if s == b:
                    spread = jnp.where(tri, spread, -1e30)
                score = jnp.dot(q, kt_ref[at, cols], preferred_element_type=F32)
                weight = (jnp.exp(spread) * score).astype(BF16)
                acc = acc + jnp.dot(weight, v_ref[cols, at], preferred_element_type=F32)
            inside[rows, at] = acc
        return carry

    lax.fori_loop(0, HALF // BLK, queries, 0)
    lax.fori_loop(0, HEADS // 2, attend, 0)

    head = c * 2 + zh // (HZ // 2)

    def arrive(k):
        @pl.when(z != k)
        def _():
            dz_from(k).wait_recv()
            zs_from(k).wait_recv()

    def advance(state, k):
        return jnp.exp(dl_chip[k, pl.ds(head, 1), :]) * state + p1[k].astype(F32)

    def zg(r):
        return pltpu.make_async_remote_copy(
            pre.at[lax.rem(zh + r, HZ)], c2.at[piece_at], zg_s.at[r], zg_r.at[r],
            device_id=chip(along(r)), device_id_type=MESH,
        )

    def gather(r, what):
        @pl.when(along(r) != 0)
        def _():
            what(zg(r))

    @pl.when(lower)
    def _():
        for k in range(HZ - 1):
            arrive(k)

        @pl.when(z < HZ - 1)
        def _():
            dz_from(HZ - 1).wait_recv()

        state = jnp.zeros((STATE_PIECE, HD), F32)
        for k in range(HZ - 1):
            pre[k] = state.astype(BF16)
            state = advance(state, k)
        pre[HZ - 1] = state.astype(BF16)

    @pl.when(jnp.logical_not(lower))
    def _():
        for k in range(NZ - 1):
            arrive(k)

        @pl.when(z < NZ - 1)
        def _():
            dz_from(NZ - 1).wait_recv()

        state = jnp.zeros((STATE_PIECE, HD), F32)
        for k in range(NZ - 1):
            if k >= HZ:
                pre[k - HZ] = state.astype(BF16)
            state = advance(state, k)
        pre[HZ - 1] = state.astype(BF16)

    for r in ZH:
        gather(r, lambda copy: copy.start())
    c2[piece_at, :] = pre[zh]
    lax.fori_loop(HEADS // 2, HEADS, attend, 0)
    for r in XY:
        ag(r).wait_send()

    @pl.when(zh < HZ - 1)
    def _():
        for r in ZH:
            zs(along(r), r).wait_send()

    @pl.when(lower)
    def _():
        for r in range(HZ):
            dz(HZ + lax.rem(z + r, HZ), HZ + r).wait_send()
            zs(HZ + lax.rem(z + r, HZ), HZ + r).wait_send()

    @pl.when(z != 0)
    def _():
        for r in ZH:
            zg(r).wait_recv()

    @pl.when(z == 0)
    def _():
        c2[...] = jnp.zeros_like(c2)

    for e in range(2):
        rows = pl.ds(e * HD, HD)
        at = pl.ds(pl.multiple_of(c * PAIR + e * HD, HD), HD)
        own = loc[at, :]
        before = c2[rows, :].astype(F32)
        even_decay = jnp.where(even, per_row(dl_own, e), per_row(dl_peer, e))
        after = even_decay * before + jnp.where(even, own, loc_recv[rows, :].astype(F32))
        loc_send[rows, :] = jnp.where(even, after, before).astype(BF16)
        here = jnp.where(even, before, after)
        carried[at, :] = here.astype(BF16)
        st_v[at, :] = per_row(dl_own, e) * here + own
    swap_carried = pltpu.make_async_remote_copy(
        loc_send, carried.at[ours], core_s.at[2], core_r.at[2],
        device_id=peer, device_id_type=MESH,
    )
    swap_carried.start()

    def write(pair, b, slot):
        rows = pl.ds(b * BLK, BLK)
        lanes = pl.ds(pl.multiple_of(pair * PAIR, PAIR), PAIR)
        return pltpu.make_async_copy(
            out_v.at[rows, lanes], out_hbm.at[rows, lanes], out_sem.at[slot]
        )

    def finish(pair, slot):
        for b in range(TOK // BLK):
            rows = pl.ds(b * BLK, BLK)
            for e in range(2):
                at = pl.ds(pl.multiple_of(pair * PAIR + e * HD, HD), HD)
                att = inside[rows, at] + jnp.dot(
                    qs_ref[rows, at], carried[at, :], preferred_element_type=F32
                )
                square = jnp.mean(att * att, axis=-1, keepdims=True)
                out_v[rows, at] = (
                    att * lax.rsqrt(square + 1e-6) * gain[pl.ds(pair * 2 + e, 1), :]
                ).astype(BF16)
            write(pair, b, slot * 4 + b).start()

    finish(c, 0)
    swap_carried.wait()
    for e in range(2):
        at = pl.ds(pl.multiple_of((1 - c) * PAIR + e * HD, HD), HD)
        decay = jnp.exp(dl_own[pl.ds((1 - c) * 2 + e, 1), :])
        st_v[at, :] = decay * carried[at, :].astype(F32) + loc[at, :]
    store_state = pltpu.make_async_copy(st_v, st_hbm, st_sem)
    store_state.start()
    finish(1 - c, 1)
    for r in ZH:
        gather(r, lambda copy: copy.wait_send())
    for b in range(TOK // BLK):
        write(c, b, b).wait()
        write(1 - c, b, 4 + b).wait()
    store_state.wait()


def local(hidden, base, down, up, decay, gain):
    anyspace = pl.BlockSpec(memory_space=pl.ANY)
    dma = pltpu.SemaphoreType.DMA
    scratch = [
        pltpu.VMEM((TOK, GROUP), BF16),
        pltpu.VMEM((3, TOK, WIDTH), BF16),
        pltpu.VMEM((3 * RANK, GROUP), BF16),
        pltpu.VMEM((3, 3 * RANK, WIDTH), BF16),
        pltpu.VMEM((HEADS, TOK), F32),
        pltpu.VMEM((HEADS, HD), F32),
        pltpu.VMEM((HALF, 2 * RANK), BF16),
        pltpu.VMEM((NTP, LORA_PIECE, 2 * RANK), BF16),
        pltpu.VMEM((HALF, 2 * RANK), BF16),
        pltpu.VMEM((8, TOK), F32),
        pltpu.VMEM((8, TOK), F32),
        pltpu.VMEM((HEADS, TOK, HD), F32),
        pltpu.VMEM((8, HD), F32),
        pltpu.VMEM((8, HD), F32),
        pltpu.VMEM((NZ, 8, HD), F32),
        pltpu.VMEM((TOK, WIDTH), BF16),
        pltpu.VMEM((TOK, WIDTH), BF16),
        pltpu.VMEM((WIDTH, TOK), BF16),
        pltpu.VMEM((TOK, WIDTH), BF16),
        pltpu.VMEM((TOK, WIDTH), F32),
        pltpu.VMEM((TOK, WIDTH), BF16),
        pltpu.VMEM((WIDTH, HD), F32),
        pltpu.VMEM((PAIR, HD), BF16),
        pltpu.VMEM((PAIR, HD), BF16),
        pltpu.VMEM((PAIR, HD), BF16),
        pltpu.VMEM((NZ, STATE_PIECE, HD), BF16),
        pltpu.VMEM((HZ, STATE_PIECE, HD), BF16),
        pltpu.VMEM((PAIR, HD), BF16),
        pltpu.VMEM((WIDTH, HD), BF16),
        pltpu.VMEM((WIDTH, HD), F32),
        dma((6,)), dma((8,)), dma,
        dma((NTP,)), dma((NTP,)), dma((NTP,)), dma((NTP,)),
        dma((NZ,)), dma((NZ,)), dma((NZ,)), dma((NZ,)), dma((NZ,)), dma((NZ,)),
        dma((3,)), dma((3,)), pltpu.SemaphoreType.REGULAR, pltpu.SemaphoreType.REGULAR,
    ]
    mixed, states = pl.pallas_call(
        kernel,
        out_shape=(
            jax.ShapeDtypeStruct((TOK, WIDTH), BF16),
            jax.ShapeDtypeStruct((WIDTH, HD), F32),
        ),
        in_specs=[anyspace] * 6,
        out_specs=(anyspace, anyspace),
        scratch_shapes=scratch,
        compiler_params=pltpu.CompilerParams(
            collective_id=0, has_side_effects=True, vmem_limit_bytes=48 * 1024 * 1024
        ),
        cost_estimate=pl.CostEstimate(
            flops=3_000_000_000, bytes_accessed=6_000_000, transcendentals=6_000_000
        ),
    )(*[pltpu.with_memory_space_constraint(a, pltpu.HBM) for a in (hidden, base, down.T, up, decay.T, gain.reshape(HEADS, HD))])
    return mixed, states.reshape(1, HEADS, HD, HD)


def solution(mesh):
    in_specs = (
        P("ctx", "tp"),
        P(None, "ctx", "tp"),
        P("tp", None),
        P(None, None, "tp"),
        P("ctx", "tp"),
        P("tp"),
    )
    out_specs = (P("ctx", "tp"), P("ctx", "tp", None, None))
    return jax.shard_map(local, mesh=mesh, in_specs=in_specs, out_specs=out_specs, check_vma=False)
```

```python
import jax
import jax.numpy as jnp
from jax import lax
from jax.experimental import pallas as pl
from jax.experimental.pallas import tpu as pltpu
from jax.sharding import PartitionSpec as P

HD = 128
HEADS = 4
TOK = 1024
HALF = 512
RANK = 64
GROUP = 384
WIDTH = HEADS * HD
PAIR = 2 * HD
BLK = 256
NX, NY, NZ = 4, 4, 16
NTP = NX * NY
LORA_PIECE = HALF // NTP
CHUNK = HALF // NX
HZ = NZ // 2
OWNERS = 4
FIRST = 2
EARLY = 5
STATE_PIECE = PAIR // OWNERS
LANES = HD // HEADS
MESH = pl.DeviceIdType.MESH
F32, BF16 = jnp.float32, jnp.bfloat16


def ring(offset, size):
    return min(offset, size - offset)


XY = sorted(range(1, NTP), key=lambda r: -(ring(r // NY, NX) + ring(r % NY, NY)))
ZH = [4, 3, 5, 2, 6, 1, 7]


def order(z):
    return jnp.where(z < HZ, z, jnp.where(z >= 12, 23 - z, z + 4))


ORDER = [z if z < HZ else (23 - z if z >= 12 else z + 4) for z in range(NZ)]


def silu(v):
    half = 0.5 * v
    return half + half * jnp.tanh(half)


def kernel(
    hid_hbm, base_hbm, dwn_hbm, up_hbm, dec_hbm, gain_hbm,
    out_v, st_v,
    hid, base, dpad, upad, dec, gain,
    part, rsum, lora,
    cum, wgt, ccol, dl_own, dl_peer, dl_chip, chip_decay,
    q_ref, qs_ref, kt_ref, v_ref, inside,
    loc, loc_send, loc_recv, tot, p1, pre, c2, carried,
    in_sem,
    rs_s, rs_r, ag_s, ag_r, zs_s, zs_r, zg_s, zg_r, dz_s, dz_r, core_s, core_r, near_sem, far_sem,
):
    ctx, tp = lax.axis_index("ctx"), lax.axis_index("tp")
    z, c = ctx // 2, ctx % 2
    x, y = tp // NY, tp % NY
    peer = {"ctx": z * 2 + (1 - c)}

    def plane(r):
        return {"tp": lax.rem(x + r // NY, NX) * NY + lax.rem(y + r % NY, NY)}

    zh = z % HZ
    base_z = z - zh
    lower = z < HZ

    def chip(other):
        return {"ctx": other * 2 + c}

    def along(r):
        return base_z + lax.rem(zh + r, HZ)

    place = order(z)
    barrier = pltpu.get_barrier_semaphore()
    for r in XY:
        pl.semaphore_signal(barrier, inc=1, device_id=plane(r), device_id_type=MESH)
    pl.semaphore_signal(barrier, inc=1, device_id=peer, device_id_type=MESH)
    for k in range(NZ):
        @pl.when(place < ORDER[k])
        def _(k=k):
            pl.semaphore_signal(barrier, inc=1, device_id=chip(k), device_id_type=MESH)

    loads = [
        pltpu.make_async_copy(dwn_hbm, dpad.at[pl.ds(RANK, RANK)], in_sem.at[0]),
        pltpu.make_async_copy(hid_hbm, hid, in_sem.at[1]),
        pltpu.make_async_copy(dec_hbm, dec, in_sem.at[2]),
        pltpu.make_async_copy(up_hbm, upad.at[:, pl.ds(RANK, RANK)], in_sem.at[3]),
        pltpu.make_async_copy(base_hbm, base, in_sem.at[4]),
        pltpu.make_async_copy(gain_hbm, gain, in_sem.at[5]),
    ]
    for load in loads:
        load.start()

    zeros = jnp.zeros((RANK, GROUP), BF16)
    dpad[pl.ds(0, RANK), :] = zeros
    dpad[pl.ds(2 * RANK, RANK), :] = zeros
    zeros = jnp.zeros((RANK, WIDTH), BF16)
    for i in range(3):
        upad[i, pl.ds(0, RANK), :] = zeros
        upad[i, pl.ds(2 * RANK, RANK), :] = zeros

    loads[0].wait()
    loads[1].wait()
    trans_b = (((1,), (1,)), ((), ()))
    for i in range(2):
        rows = pl.ds(i * BLK, BLK)
        mine = lax.dot_general(
            hid[rows, :], dpad[pl.ds(RANK, 2 * RANK), :], trans_b, preferred_element_type=F32
        ) + lax.dot_general(
            hid[pl.ds(HALF + i * BLK, BLK), :], dpad[pl.ds(0, 2 * RANK), :], trans_b,
            preferred_element_type=F32,
        )
        part[rows, :] = mine.astype(BF16)

    pl.semaphore_wait(barrier, NTP - 1 + 1 + place)

    def rs(r):
        to = plane(r)
        return pltpu.make_async_remote_copy(
            part.at[pl.ds(pl.multiple_of(to["tp"] * LORA_PIECE, LORA_PIECE), LORA_PIECE)],
            rsum.at[r], rs_s.at[r], rs_r.at[r], device_id=to, device_id_type=MESH,
        )

    for r in XY:
        rs(r).start()

    for k in range(NZ):
        same = lower if k < HZ else jnp.logical_not(lower)

        @pl.when(jnp.logical_and(place > ORDER[k], same))
        def _(k=k):
            pl.semaphore_signal(near_sem, inc=1, device_id=chip(k), device_id_type=MESH)

        @pl.when(jnp.logical_and(place > ORDER[k], jnp.logical_and(jnp.logical_not(same), k >= FIRST)))
        def _(k=k):
            pl.semaphore_signal(far_sem, inc=1, device_id=chip(k), device_id_type=MESH)

    loads[2].wait()
    run = jnp.concatenate([dec[...], jnp.zeros((8 - HEADS, TOK), F32)], axis=0)
    lane = lax.broadcasted_iota(jnp.int32, (8, TOK), 1)
    step = 1
    while step < TOK:
        run = run + jnp.where(lane >= step, pltpu.roll(run, step, 1), 0.0)
        step *= 2
    last = run[:, TOK - 1 :]
    cum[...] = run
    wgt[...] = jnp.exp(last - run)
    dl_own[...] = jnp.broadcast_to(last, (8, HD))
    swap_decay = pltpu.make_async_remote_copy(
        dl_own, dl_peer, core_s.at[0], core_r.at[0], device_id=peer, device_id_type=MESH
    )
    swap_decay.start()

    def ccol_of(h, carry):
        ccol[h] = jnp.broadcast_to(cum[pl.ds(h, 1), :], (HD, TOK)).T
        return carry

    lax.fori_loop(0, HEADS, ccol_of, 0)

    swap_decay.wait()
    head_of_lane = lax.broadcasted_iota(jnp.int32, (8, HD), 1) // LANES
    dl_chip[z] = jnp.sum(
        jnp.where(
            head_of_lane == lax.broadcasted_iota(jnp.int32, (8, HD), 0),
            dl_own[...] + dl_peer[...], 0.0,
        ),
        axis=0, keepdims=True,
    )

    def dz(owner):
        return pltpu.make_async_remote_copy(
            dl_chip.at[z], dl_chip.at[z], dz_s.at[owner], dz_r.at[z],
            device_id=chip(owner), device_id_type=MESH,
        )

    def dz_from(k):
        return pltpu.make_async_remote_copy(
            dl_chip.at[k], dl_chip.at[k], dz_s.at[0], dz_r.at[k],
            device_id=peer, device_id_type=MESH,
        )

    def to_owners(half, what):
        for k in range(OWNERS):
            owner = half + FIRST + jnp.where(lower, k, OWNERS - 1 - k)

            @pl.when(owner != z)
            def _(owner=owner, k=k):
                what(owner, k)

    mine_at = pl.ds(pl.multiple_of(tp * LORA_PIECE, LORA_PIECE), LORA_PIECE)
    for r in XY:
        rs(r).wait_recv()
    total = part[mine_at, :].astype(F32)
    for r in range(1, NTP):
        total = total + rsum[r].astype(F32)
    lora[mine_at, :] = total.astype(BF16)

    def ag(r):
        return pltpu.make_async_remote_copy(
            lora.at[mine_at], lora.at[mine_at], ag_s.at[r], ag_r.at[r],
            device_id=plane(r), device_id_type=MESH,
        )

    for r in XY:
        ag(r).start()
    for r in XY:
        rs(r).wait_send()
    later = jnp.where(lower, HZ, NZ) - 1 - place

    @pl.when(later > 0)
    def _():
        pl.semaphore_wait(near_sem, later)

    adds = zh < HZ - 1

    @pl.when(adds)
    def _():
        to_owners(base_z, lambda owner, k: dz(owner).start())

    loads[3].wait()
    loads[4].wait()
    loads[5].wait()

    def projected(i, a, row, size, lanes):
        return base[i, pl.ds(a * HALF + row, size), lanes].astype(F32) + jnp.dot(
            lora[pl.ds(row, size), :],
            upad[i, pl.ds(RANK - RANK * a, 2 * RANK), lanes],
            preferred_element_type=F32,
        )

    for n, shift in enumerate((0, 1, 3, 2)):
        for ry in range(NY):
            if shift or ry:
                ag(shift * NY + ry).wait_recv()
        row = pl.multiple_of(lax.rem(x + NX - shift, NX) * CHUNK, CHUNK)
        scaled = []
        for a in range(2):
            at = pl.ds(pl.multiple_of(a * HALF + row, CHUNK), CHUNK)
            k = silu(projected(1, a, row, CHUNK, slice(None))).astype(BF16).T
            kt_ref[:, at] = k
            v_ref[at, :] = projected(2, a, row, CHUNK, slice(None)).astype(BF16)
            scaled.append(
                [
                    (k[h * HD : (h + 1) * HD].astype(F32) * wgt[h : h + 1, at]).astype(BF16)
                    for h in range(HEADS)
                ]
            )
        for h in range(HEADS):
            lanes = slice(h * HD, (h + 1) * HD)
            part_sum = sum(
                jnp.dot(
                    scaled[a][h],
                    v_ref[pl.ds(pl.multiple_of(a * HALF + row, CHUNK), CHUNK), lanes],
                    preferred_element_type=F32,
                )
                for a in range(2)
            )
            if n == 0:
                loc[lanes, :] = part_sum
            else:
                loc[lanes, :] += part_sum

    ours = pl.ds(pl.multiple_of(c * PAIR, PAIR), PAIR)
    theirs = pl.ds(pl.multiple_of((1 - c) * PAIR, PAIR), PAIR)
    even = c == 0

    loc_send[...] = loc[theirs, :].astype(BF16)
    swap_local = pltpu.make_async_remote_copy(
        loc_send, loc_recv, core_s.at[1], core_r.at[1], device_id=peer, device_id_type=MESH
    )
    swap_local.start()
    @pl.when(adds)
    def _():
        to_owners(base_z, lambda owner, k: dz(owner).wait_send())

    swap_local.wait()

    def per_row(ref, e):
        return jnp.exp(ref[pl.ds(c * 2 + e, 1), :])

    for e in range(2):
        rows = pl.ds(e * HD, HD)
        own = loc[pl.ds(pl.multiple_of(c * PAIR + e * HD, HD), HD), :]
        other = loc_recv[rows, :].astype(F32)
        odd_decay = jnp.where(even, per_row(dl_peer, e), per_row(dl_own, e))
        tot[rows, :] = (
            jnp.where(even, own, other) * odd_decay + jnp.where(even, other, own)
        ).astype(BF16)

    def zs(owner, k):
        return pltpu.make_async_remote_copy(
            tot.at[pl.ds(k * STATE_PIECE, STATE_PIECE)], p1.at[z], zs_s.at[owner], zs_r.at[z],
            device_id=chip(owner), device_id_type=MESH,
        )

    def zs_from(k):
        return pltpu.make_async_remote_copy(
            tot.at[pl.ds(0, STATE_PIECE)], p1.at[k], zs_s.at[0], zs_r.at[k],
            device_id=peer, device_id_type=MESH,
        )

    @pl.when(adds)
    def _():
        to_owners(base_z, lambda owner, k: zs(owner, k).start())

    far = jnp.logical_and(lower, z >= EARLY)

    def to_far(what):
        for k in range(OWNERS):
            what(HZ + FIRST + OWNERS - 1 - k, k)

    @pl.when(far)
    def _():
        pl.semaphore_wait(far_sem, HZ)

        def start(owner, k):
            dz(owner).start()
            zs(owner, k).start()

        to_far(start)

    owns = jnp.logical_and(zh >= FIRST, zh < FIRST + OWNERS)
    mine_k = jnp.where(lower, zh - FIRST, FIRST + OWNERS - 1 - zh)
    mine_k = jnp.clip(mine_k, 0, OWNERS - 1)
    piece_at = pl.ds(pl.multiple_of(mine_k * STATE_PIECE, STATE_PIECE), STATE_PIECE)

    def queries(i, carry):
        for a in range(2):
            row = pl.multiple_of(i * BLK, BLK)
            rows = pl.ds(a * HALF + row, BLK)
            q = silu(projected(0, a, row, BLK, slice(None))).astype(BF16)
            q_ref[rows, :] = q
            for h in range(HEADS):
                grow = jnp.exp(ccol[h, rows, :])
                qs_ref[rows, h * HD : (h + 1) * HD] = (
                    q[:, h * HD : (h + 1) * HD].astype(F32) * grow
                ).astype(BF16)
        return carry

    tri = lax.broadcasted_iota(jnp.int32, (BLK, BLK), 0) >= lax.broadcasted_iota(
        jnp.int32, (BLK, BLK), 1
    )

    def attend(h, carry):
        at = pl.ds(pl.multiple_of(h * HD, HD), HD)
        for b in range(TOK // BLK):
            rows = pl.ds(b * BLK, BLK)
            q = q_ref[rows, at]
            col = ccol[h, rows, :]
            col = jnp.concatenate([col, col], axis=1)
            acc = jnp.zeros((BLK, HD), F32)
            for s in range(b + 1):
                cols = pl.ds(s * BLK, BLK)
                spread = col - cum[pl.ds(h, 1), cols]
                if s == b:
                    spread = jnp.where(tri, spread, -1e30)
                score = jnp.dot(q, kt_ref[at, cols], preferred_element_type=F32)
                weight = (jnp.exp(spread) * score).astype(BF16)
                acc = acc + jnp.dot(weight, v_ref[cols, at], preferred_element_type=F32)
            inside[rows, at] = acc
        return carry

    scan_first = jnp.logical_or(z == 4, z == 5)
    blocks_before = jnp.where(scan_first, 0, HALF // BLK)
    heads_before = jnp.where(scan_first, 0, HEADS // 2)
    lax.fori_loop(0, blocks_before, queries, 0)
    lax.fori_loop(0, heads_before, attend, 0)

    head_lane = (c * 2 + mine_k // 2) * LANES
    lane_of = lax.broadcasted_iota(jnp.int32, (1, 1, HD), 2)

    def arrive(k):
        @pl.when(z != k)
        def _():
            zs_from(k).wait_recv()

    def decays(first, last):
        for k in range(first, last):
            @pl.when(z != k)
            def _(k=k):
                dz_from(k).wait_recv()

        log = jnp.sum(
            jnp.where(lane_of == head_lane, dl_chip[first:last], 0.0), axis=2, keepdims=True
        )
        chip_decay[first:last] = jnp.broadcast_to(jnp.exp(log), (last - first, 1, HD))

    def advance(state, k):
        return chip_decay[k] * state + p1[k].astype(F32)

    def zg(b):
        return pltpu.make_async_remote_copy(
            pre.at[b % HZ], c2.at[piece_at], zg_s.at[b % HZ], zg_r.at[mine_k],
            device_id=chip(b), device_id_type=MESH,
        )

    def zg_from(k):
        rows = pl.ds(k * STATE_PIECE, STATE_PIECE)
        return pltpu.make_async_remote_copy(
            pre.at[0], c2.at[rows], zg_s.at[0], zg_r.at[k], device_id=peer, device_id_type=MESH
        )

    def give(b):
        @pl.when(z != b)
        def _():
            zg(b).start()

    def given(blocks):
        for b in blocks:
            @pl.when(z != b)
            def _(b=b):
                zg(b).wait_send()

    def early():
        return pltpu.make_async_remote_copy(
            pre.at[EARLY], p1.at[EARLY - 1], zs_s.at[0], zs_r.at[EARLY - 1],
            device_id=chip(NZ - 1 - z), device_id_type=MESH,
        )

    @pl.when(jnp.logical_and(owns, lower))
    def _():
        p1[z] = tot[piece_at, :]
        decays(0, HZ - 1)
        state = jnp.zeros((STATE_PIECE, HD), F32)
        for k in range(HZ - 1):
            arrive(k)
            state = advance(state, k)
            pre[k + 1] = state.astype(BF16)
            give(k + 1)
            if k == EARLY - 1:
                @pl.when(jnp.logical_not(far))
                def _():
                    pl.semaphore_wait(far_sem, HZ)

                early().start()

    @pl.when(jnp.logical_and(owns, jnp.logical_not(lower)))
    def _():
        p1[z] = tot[piece_at, :]
        decays(EARLY, NZ - 1)
        zs_from(EARLY - 1).wait_recv()
        state = p1[EARLY - 1].astype(F32)
        for k in range(EARLY, NZ - 1):
            arrive(k)
            state = advance(state, k)
            if k >= HZ - 1:
                pre[k + 1 - HZ] = state.astype(BF16)
        for b in (15, 8, 14, 9, 13, 12, 10, 11):
            give(b)

    @pl.when(owns)
    def _():
        c2[piece_at, :] = pre[zh]

    lax.fori_loop(blocks_before, HALF // BLK, queries, 0)
    lax.fori_loop(heads_before, HEADS, attend, 0)
    for r in XY:
        ag(r).wait_send()

    @pl.when(adds)
    def _():
        to_owners(base_z, lambda owner, k: zs(owner, k).wait_send())

    @pl.when(far)
    def _():
        def sent(owner, k):
            dz(owner).wait_send()
            zs(owner, k).wait_send()

        to_far(sent)

    @pl.when(z != 0)
    def _():
        to_owners(base_z, lambda owner, k: zg_from(k).wait_recv())

    @pl.when(z == 0)
    def _():
        c2[...] = jnp.zeros_like(c2)

    for e in range(2):
        rows = pl.ds(e * HD, HD)
        at = pl.ds(pl.multiple_of(c * PAIR + e * HD, HD), HD)
        own = loc[at, :]
        before = c2[rows, :].astype(F32)
        even_decay = jnp.where(even, per_row(dl_own, e), per_row(dl_peer, e))
        after = even_decay * before + jnp.where(even, own, loc_recv[rows, :].astype(F32))
        loc_send[rows, :] = jnp.where(even, after, before).astype(BF16)
        here = jnp.where(even, before, after)
        carried[at, :] = here.astype(BF16)
        st_v[at, :] = per_row(dl_own, e) * here + own
    swap_carried = pltpu.make_async_remote_copy(
        loc_send, carried.at[ours], core_s.at[2], core_r.at[2],
        device_id=peer, device_id_type=MESH,
    )
    swap_carried.start()

    def finish(pair):
        for b in range(TOK // BLK):
            rows = pl.ds(b * BLK, BLK)
            for e in range(2):
                at = pl.ds(pl.multiple_of(pair * PAIR + e * HD, HD), HD)
                att = inside[rows, at] + jnp.dot(
                    qs_ref[rows, at], carried[at, :], preferred_element_type=F32
                )
                square = jnp.mean(att * att, axis=-1, keepdims=True)
                out_v[rows, at] = (
                    att * lax.rsqrt(square + 1e-6) * gain[pl.ds(pair * 2 + e, 1), :]
                ).astype(BF16)

    finish(c)
    swap_carried.wait()
    for e in range(2):
        at = pl.ds(pl.multiple_of((1 - c) * PAIR + e * HD, HD), HD)
        decay = jnp.exp(dl_own[pl.ds((1 - c) * 2 + e, 1), :])
        st_v[at, :] = decay * carried[at, :].astype(F32) + loc[at, :]
    finish(1 - c)

    @pl.when(jnp.logical_and(owns, lower))
    def _():
        given(range(1, HZ))
        early().wait_send()

    @pl.when(jnp.logical_and(owns, jnp.logical_not(lower)))
    def _():
        given(range(HZ, NZ))


def local(hidden, base, down, up, decay, gain):
    anyspace = pl.BlockSpec(memory_space=pl.ANY)
    dma = pltpu.SemaphoreType.DMA
    scratch = [
        pltpu.VMEM((TOK, GROUP), BF16),
        pltpu.VMEM((3, TOK, WIDTH), BF16),
        pltpu.VMEM((3 * RANK, GROUP), BF16),
        pltpu.VMEM((3, 3 * RANK, WIDTH), BF16),
        pltpu.VMEM((HEADS, TOK), F32),
        pltpu.VMEM((HEADS, HD), F32),
        pltpu.VMEM((HALF, 2 * RANK), BF16),
        pltpu.VMEM((NTP, LORA_PIECE, 2 * RANK), BF16),
        pltpu.VMEM((HALF, 2 * RANK), BF16),
        pltpu.VMEM((8, TOK), F32),
        pltpu.VMEM((8, TOK), F32),
        pltpu.VMEM((HEADS, TOK, HD), F32),
        pltpu.VMEM((8, HD), F32),
        pltpu.VMEM((8, HD), F32),
        pltpu.VMEM((NZ, 1, HD), F32),
        pltpu.VMEM((NZ, 1, HD), F32),
        pltpu.VMEM((TOK, WIDTH), BF16),
        pltpu.VMEM((TOK, WIDTH), BF16),
        pltpu.VMEM((WIDTH, TOK), BF16),
        pltpu.VMEM((TOK, WIDTH), BF16),
        pltpu.VMEM((TOK, WIDTH), F32),
        pltpu.VMEM((WIDTH, HD), F32),
        pltpu.VMEM((PAIR, HD), BF16),
        pltpu.VMEM((PAIR, HD), BF16),
        pltpu.VMEM((PAIR, HD), BF16),
        pltpu.VMEM((NZ, STATE_PIECE, HD), BF16),
        pltpu.VMEM((HZ, STATE_PIECE, HD), BF16),
        pltpu.VMEM((PAIR, HD), BF16),
        pltpu.VMEM((WIDTH, HD), BF16),
        dma((6,)),
        dma((NTP,)), dma((NTP,)), dma((NTP,)), dma((NTP,)),
        dma((NZ,)), dma((NZ,)), dma((NZ,)), dma((NZ,)), dma((NZ,)), dma((NZ,)),
        dma((3,)), dma((3,)), pltpu.SemaphoreType.REGULAR, pltpu.SemaphoreType.REGULAR,
    ]
    mixed, states = pl.pallas_call(
        kernel,
        out_shape=(
            jax.ShapeDtypeStruct((TOK, WIDTH), BF16),
            jax.ShapeDtypeStruct((WIDTH, HD), F32),
        ),
        in_specs=[anyspace] * 6,
        out_specs=(pl.BlockSpec(memory_space=pltpu.VMEM),) * 2,
        scratch_shapes=scratch,
        compiler_params=pltpu.CompilerParams(
            collective_id=0, has_side_effects=True, vmem_limit_bytes=48 * 1024 * 1024
        ),
        cost_estimate=pl.CostEstimate(
            flops=3_000_000_000, bytes_accessed=6_000_000, transcendentals=6_000_000
        ),
    )(*[pltpu.with_memory_space_constraint(a, pltpu.HBM) for a in (hidden, base, down.T, up, decay.T, gain.reshape(HEADS, HD))])
    return mixed, states.reshape(1, HEADS, HD, HD)


def solution(mesh):
    in_specs = (
        P("ctx", "tp"),
        P(None, "ctx", "tp"),
        P("tp", None),
        P(None, None, "tp"),
        P("ctx", "tp"),
        P("tp"),
    )
    out_specs = (P("ctx", "tp"), P("ctx", "tp", None, None))
    return jax.shard_map(local, mesh=mesh, in_specs=in_specs, out_specs=out_specs, check_vma=False)
```

```python
import jax
import jax.numpy as jnp
from jax import lax
from jax.experimental import pallas as pl
from jax.experimental.pallas import tpu as pltpu
from jax.sharding import PartitionSpec as P

HD = 128
HEADS = 4
TOK = 1024
HALF = 512
RANK = 64
GROUP = 384
WIDTH = HEADS * HD
PAIR = 2 * HD
BLK = 256
NX, NY, NZ = 4, 4, 16
NTP = NX * NY
LORA_PIECE = HALF // NTP
CHUNK = HALF // NX
HZ = NZ // 2
OWNERS = 4
FIRST = 2
EARLY = 7
STATE_PIECE = PAIR // OWNERS
LANES = HD // HEADS
MESH = pl.DeviceIdType.MESH
F32, BF16 = jnp.float32, jnp.bfloat16


def ring(offset, size):
    return min(offset, size - offset)


XY = sorted(range(1, NTP), key=lambda r: -(ring(r // NY, NX) + ring(r % NY, NY)))
ZH = [4, 3, 5, 2, 6, 1, 7]


def order(z):
    return jnp.where(z < HZ, z, jnp.where(z >= 12, 23 - z, z + 4))


CROSS = [*range(FIRST, FIRST + OWNERS), *range(max(EARLY, FIRST + OWNERS), HZ)]
ORDER = [z if z < HZ else (23 - z if z >= 12 else z + 4) for z in range(NZ)]


def silu(v):
    half = 0.5 * v
    return half + half * jnp.tanh(half)


def kernel(
    hid_hbm, base_hbm, dwn_hbm, up_hbm, dec_hbm, gain_hbm,
    out_v, st_v,
    hid, base, dpad, upad, dec, gain,
    part, rsum, lora,
    cum, wgt, ccol, dl_own, dl_peer, dl_chip, chip_decay,
    q_ref, qs_ref, kt_ref, v_ref, inside,
    loc, loc_send, loc_recv, tot, p1, pre, c2, carried,
    in_sem,
    rs_s, rs_r, ag_s, ag_r, zs_s, zs_r, zg_s, zg_r, dz_s, dz_r, core_s, core_r, near_sem, far_sem,
):
    ctx, tp = lax.axis_index("ctx"), lax.axis_index("tp")
    z, c = ctx // 2, ctx % 2
    x, y = tp // NY, tp % NY
    peer = {"ctx": z * 2 + (1 - c)}

    def plane(r):
        return {"tp": lax.rem(x + r // NY, NX) * NY + lax.rem(y + r % NY, NY)}

    zh = z % HZ
    base_z = z - zh
    lower = z < HZ

    def chip(other):
        return {"ctx": other * 2 + c}

    def along(r):
        return base_z + lax.rem(zh + r, HZ)

    place = order(z)
    barrier = pltpu.get_barrier_semaphore()
    for r in XY:
        pl.semaphore_signal(barrier, inc=1, device_id=plane(r), device_id_type=MESH)
    pl.semaphore_signal(barrier, inc=1, device_id=peer, device_id_type=MESH)
    for k in range(NZ):
        @pl.when(place < ORDER[k])
        def _(k=k):
            pl.semaphore_signal(barrier, inc=1, device_id=chip(k), device_id_type=MESH)

    loads = [
        pltpu.make_async_copy(dwn_hbm, dpad.at[pl.ds(RANK, RANK)], in_sem.at[0]),
        pltpu.make_async_copy(hid_hbm, hid, in_sem.at[1]),
        pltpu.make_async_copy(dec_hbm, dec, in_sem.at[2]),
        pltpu.make_async_copy(up_hbm, upad.at[:, pl.ds(RANK, RANK)], in_sem.at[3]),
        pltpu.make_async_copy(base_hbm, base, in_sem.at[4]),
        pltpu.make_async_copy(gain_hbm, gain, in_sem.at[5]),
    ]
    for load in loads:
        load.start()

    zeros = jnp.zeros((RANK, GROUP), BF16)
    dpad[pl.ds(0, RANK), :] = zeros
    dpad[pl.ds(2 * RANK, RANK), :] = zeros
    zeros = jnp.zeros((RANK, WIDTH), BF16)
    for i in range(3):
        upad[i, pl.ds(0, RANK), :] = zeros
        upad[i, pl.ds(2 * RANK, RANK), :] = zeros

    loads[0].wait()
    loads[1].wait()
    trans_b = (((1,), (1,)), ((), ()))
    for i in range(2):
        rows = pl.ds(i * BLK, BLK)
        mine = lax.dot_general(
            hid[rows, :], dpad[pl.ds(RANK, 2 * RANK), :], trans_b, preferred_element_type=F32
        ) + lax.dot_general(
            hid[pl.ds(HALF + i * BLK, BLK), :], dpad[pl.ds(0, 2 * RANK), :], trans_b,
            preferred_element_type=F32,
        )
        part[rows, :] = mine.astype(BF16)

    pl.semaphore_wait(barrier, NTP - 1 + 1 + place)

    def rs(r):
        to = plane(r)
        return pltpu.make_async_remote_copy(
            part.at[pl.ds(pl.multiple_of(to["tp"] * LORA_PIECE, LORA_PIECE), LORA_PIECE)],
            rsum.at[r], rs_s.at[r], rs_r.at[r], device_id=to, device_id_type=MESH,
        )

    for r in XY:
        rs(r).start()

    for k in range(NZ):
        same = lower if k < HZ else jnp.logical_not(lower)

        @pl.when(jnp.logical_and(place > ORDER[k], same))
        def _(k=k):
            pl.semaphore_signal(near_sem, inc=1, device_id=chip(k), device_id_type=MESH)

        @pl.when(jnp.logical_and(place > ORDER[k], jnp.logical_and(jnp.logical_not(same), k in CROSS)))
        def _(k=k):
            pl.semaphore_signal(far_sem, inc=1, device_id=chip(k), device_id_type=MESH)

    loads[2].wait()
    run = jnp.concatenate([dec[...], jnp.zeros((8 - HEADS, TOK), F32)], axis=0)
    lane = lax.broadcasted_iota(jnp.int32, (8, TOK), 1)
    step = 1
    while step < TOK:
        run = run + jnp.where(lane >= step, pltpu.roll(run, step, 1), 0.0)
        step *= 2
    last = run[:, TOK - 1 :]
    cum[...] = run
    wgt[...] = jnp.exp(last - run)
    dl_own[...] = jnp.broadcast_to(last, (8, HD))
    swap_decay = pltpu.make_async_remote_copy(
        dl_own, dl_peer, core_s.at[0], core_r.at[0], device_id=peer, device_id_type=MESH
    )
    swap_decay.start()

    def ccol_of(h, carry):
        ccol[h] = jnp.broadcast_to(cum[pl.ds(h, 1), :], (HD, TOK)).T
        return carry

    lax.fori_loop(0, HEADS, ccol_of, 0)

    swap_decay.wait()
    head_of_lane = lax.broadcasted_iota(jnp.int32, (8, HD), 1) // LANES
    dl_chip[z] = jnp.sum(
        jnp.where(
            head_of_lane == lax.broadcasted_iota(jnp.int32, (8, HD), 0),
            dl_own[...] + dl_peer[...], 0.0,
        ),
        axis=0, keepdims=True,
    )

    def dz(owner):
        return pltpu.make_async_remote_copy(
            dl_chip.at[z], dl_chip.at[z], dz_s.at[owner], dz_r.at[z],
            device_id=chip(owner), device_id_type=MESH,
        )

    def dz_from(k):
        return pltpu.make_async_remote_copy(
            dl_chip.at[k], dl_chip.at[k], dz_s.at[0], dz_r.at[k],
            device_id=peer, device_id_type=MESH,
        )

    def to_owners(half, what):
        for k in range(OWNERS):
            owner = half + FIRST + jnp.where(lower, k, OWNERS - 1 - k)

            @pl.when(owner != z)
            def _(owner=owner, k=k):
                what(owner, k)

    mine_at = pl.ds(pl.multiple_of(tp * LORA_PIECE, LORA_PIECE), LORA_PIECE)
    for r in XY:
        rs(r).wait_recv()
    total = part[mine_at, :].astype(F32)
    for r in range(1, NTP):
        total = total + rsum[r].astype(F32)
    lora[mine_at, :] = total.astype(BF16)

    def ag(r):
        return pltpu.make_async_remote_copy(
            lora.at[mine_at], lora.at[mine_at], ag_s.at[r], ag_r.at[r],
            device_id=plane(r), device_id_type=MESH,
        )

    for r in XY:
        ag(r).start()
    for r in XY:
        rs(r).wait_send()
    later = jnp.where(lower, HZ, NZ) - 1 - place

    @pl.when(later > 0)
    def _():
        pl.semaphore_wait(near_sem, later)

    adds = jnp.logical_or(zh < HZ - 1, jnp.logical_and(lower, EARLY == HZ))

    @pl.when(adds)
    def _():
        to_owners(base_z, lambda owner, k: dz(owner).start())

    loads[3].wait()
    loads[4].wait()
    loads[5].wait()

    def projected(i, a, row, size, lanes):
        return base[i, pl.ds(a * HALF + row, size), lanes].astype(F32) + jnp.dot(
            lora[pl.ds(row, size), :],
            upad[i, pl.ds(RANK - RANK * a, 2 * RANK), lanes],
            preferred_element_type=F32,
        )

    for n, shift in enumerate((0, 1, 3, 2)):
        for ry in range(NY):
            if shift or ry:
                ag(shift * NY + ry).wait_recv()
        row = pl.multiple_of(lax.rem(x + NX - shift, NX) * CHUNK, CHUNK)
        scaled = []
        for a in range(2):
            at = pl.ds(pl.multiple_of(a * HALF + row, CHUNK), CHUNK)
            k = silu(projected(1, a, row, CHUNK, slice(None))).astype(BF16).T
            kt_ref[:, at] = k
            v_ref[at, :] = projected(2, a, row, CHUNK, slice(None)).astype(BF16)
            scaled.append(
                [
                    (k[h * HD : (h + 1) * HD].astype(F32) * wgt[h : h + 1, at]).astype(BF16)
                    for h in range(HEADS)
                ]
            )
        for h in range(HEADS):
            lanes = slice(h * HD, (h + 1) * HD)
            part_sum = sum(
                jnp.dot(
                    scaled[a][h],
                    v_ref[pl.ds(pl.multiple_of(a * HALF + row, CHUNK), CHUNK), lanes],
                    preferred_element_type=F32,
                )
                for a in range(2)
            )
            if n == 0:
                loc[lanes, :] = part_sum
            else:
                loc[lanes, :] += part_sum

    ours = pl.ds(pl.multiple_of(c * PAIR, PAIR), PAIR)
    theirs = pl.ds(pl.multiple_of((1 - c) * PAIR, PAIR), PAIR)
    even = c == 0

    loc_send[...] = loc[theirs, :].astype(BF16)
    swap_local = pltpu.make_async_remote_copy(
        loc_send, loc_recv, core_s.at[1], core_r.at[1], device_id=peer, device_id_type=MESH
    )
    swap_local.start()
    @pl.when(adds)
    def _():
        to_owners(base_z, lambda owner, k: dz(owner).wait_send())

    swap_local.wait()

    def per_row(ref, e):
        return jnp.exp(ref[pl.ds(c * 2 + e, 1), :])

    for e in range(2):
        rows = pl.ds(e * HD, HD)
        own = loc[pl.ds(pl.multiple_of(c * PAIR + e * HD, HD), HD), :]
        other = loc_recv[rows, :].astype(F32)
        odd_decay = jnp.where(even, per_row(dl_peer, e), per_row(dl_own, e))
        tot[rows, :] = (
            jnp.where(even, own, other) * odd_decay + jnp.where(even, other, own)
        ).astype(BF16)

    def zs(owner, k):
        return pltpu.make_async_remote_copy(
            tot.at[pl.ds(k * STATE_PIECE, STATE_PIECE)], p1.at[z], zs_s.at[owner], zs_r.at[z],
            device_id=chip(owner), device_id_type=MESH,
        )

    def zs_from(k):
        return pltpu.make_async_remote_copy(
            tot.at[pl.ds(0, STATE_PIECE)], p1.at[k], zs_s.at[0], zs_r.at[k],
            device_id=peer, device_id_type=MESH,
        )

    @pl.when(adds)
    def _():
        to_owners(base_z, lambda owner, k: zs(owner, k).start())

    def first():
        return pltpu.make_async_remote_copy(
            tot, c2, core_s.at[3], core_r.at[3], device_id=chip(1), device_id_type=MESH
        )

    @pl.when(z == 0)
    def _():
        first().start()

    far = jnp.logical_and(lower, z >= EARLY)

    def to_far(what):
        for k in range(OWNERS):
            what(HZ + FIRST + OWNERS - 1 - k, k)

    @pl.when(far)
    def _():
        pl.semaphore_wait(far_sem, HZ)

        def start(owner, k):
            dz(owner).start()
            zs(owner, k).start()

        to_far(start)

    owns = jnp.logical_and(zh >= FIRST, zh < FIRST + OWNERS)
    mine_k = jnp.where(lower, zh - FIRST, FIRST + OWNERS - 1 - zh)
    mine_k = jnp.clip(mine_k, 0, OWNERS - 1)
    piece_at = pl.ds(pl.multiple_of(mine_k * STATE_PIECE, STATE_PIECE), STATE_PIECE)

    def queries(i, carry):
        for a in range(2):
            row = pl.multiple_of(i * BLK, BLK)
            rows = pl.ds(a * HALF + row, BLK)
            q = silu(projected(0, a, row, BLK, slice(None))).astype(BF16)
            q_ref[rows, :] = q
            for h in range(HEADS):
                grow = jnp.exp(ccol[h, rows, :])
                qs_ref[rows, h * HD : (h + 1) * HD] = (
                    q[:, h * HD : (h + 1) * HD].astype(F32) * grow
                ).astype(BF16)
        return carry

    tri = lax.broadcasted_iota(jnp.int32, (BLK, BLK), 0) >= lax.broadcasted_iota(
        jnp.int32, (BLK, BLK), 1
    )

    def attend(h, carry):
        at = pl.ds(pl.multiple_of(h * HD, HD), HD)
        for b in range(TOK // BLK):
            rows = pl.ds(b * BLK, BLK)
            q = q_ref[rows, at]
            col = ccol[h, rows, :]
            col = jnp.concatenate([col, col], axis=1)
            acc = jnp.zeros((BLK, HD), F32)
            for s in range(b + 1):
                cols = pl.ds(s * BLK, BLK)
                spread = col - cum[pl.ds(h, 1), cols]
                if s == b:
                    spread = jnp.where(tri, spread, -1e30)
                score = jnp.dot(q, kt_ref[at, cols], preferred_element_type=F32)
                weight = (jnp.exp(spread) * score).astype(BF16)
                acc = acc + jnp.dot(weight, v_ref[cols, at], preferred_element_type=F32)
            inside[rows, at] = acc
        return carry

    heads_before = jnp.where(jnp.logical_or(z == 4, z == 5), 1, 2)
    lax.fori_loop(0, HALF // BLK, queries, 0)
    lax.fori_loop(0, heads_before, attend, 0)

    head_lane = (c * 2 + mine_k // 2) * LANES
    lane_of = lax.broadcasted_iota(jnp.int32, (1, 1, HD), 2)

    def arrive(k):
        @pl.when(z != k)
        def _():
            zs_from(k).wait_recv()

    def decays(first, last):
        for k in range(first, last):
            @pl.when(z != k)
            def _(k=k):
                dz_from(k).wait_recv()

        log = jnp.sum(
            jnp.where(lane_of == head_lane, dl_chip[first:last], 0.0), axis=2, keepdims=True
        )
        chip_decay[first:last] = jnp.broadcast_to(jnp.exp(log), (last - first, 1, HD))

    def advance(state, k):
        return chip_decay[k] * state + p1[k].astype(F32)

    def zg(b):
        return pltpu.make_async_remote_copy(
            pre.at[b % HZ], c2.at[piece_at], zg_s.at[b % HZ], zg_r.at[mine_k],
            device_id=chip(b), device_id_type=MESH,
        )

    def zg_from(k):
        rows = pl.ds(k * STATE_PIECE, STATE_PIECE)
        return pltpu.make_async_remote_copy(
            pre.at[0], c2.at[rows], zg_s.at[0], zg_r.at[k], device_id=peer, device_id_type=MESH
        )

    def give(b):
        @pl.when(z != b)
        def _():
            zg(b).start()

    def given(blocks):
        for b in blocks:
            @pl.when(z != b)
            def _(b=b):
                zg(b).wait_send()

    def early():
        return pltpu.make_async_remote_copy(
            pre.at[EARLY % HZ], p1.at[EARLY - 1], zs_s.at[0], zs_r.at[EARLY - 1],
            device_id=chip(NZ - 1 - z), device_id_type=MESH,
        )

    @pl.when(jnp.logical_and(owns, lower))
    def _():
        p1[z] = tot[piece_at, :]
        ends = max(HZ - 1, EARLY)
        decays(0, ends)
        state = jnp.zeros((STATE_PIECE, HD), F32)
        for k in range(ends):
            arrive(k)
            state = advance(state, k)
            pre[(k + 1) % HZ] = state.astype(BF16)
            if k == EARLY - 1:
                @pl.when(jnp.logical_not(far))
                def _():
                    pl.semaphore_wait(far_sem, HZ)

                early().start()
            if 1 < k + 1 < HZ:
                give(k + 1)

    @pl.when(jnp.logical_and(owns, jnp.logical_not(lower)))
    def _():
        p1[z] = tot[piece_at, :]
        decays(EARLY, NZ - 1)
        zs_from(EARLY - 1).wait_recv()
        state = p1[EARLY - 1].astype(F32)
        for k in range(EARLY, NZ - 1):
            arrive(k)
            state = advance(state, k)
            if k >= HZ - 1:
                pre[k + 1 - HZ] = state.astype(BF16)
        for b in (15, 8, 14, 9, 13, 12, 10, 11):
            give(b)

    @pl.when(owns)
    def _():
        c2[piece_at, :] = pre[zh]

    lax.fori_loop(heads_before, HEADS, attend, 0)
    for r in XY:
        ag(r).wait_send()

    @pl.when(adds)
    def _():
        to_owners(base_z, lambda owner, k: zs(owner, k).wait_send())

    @pl.when(far)
    def _():
        def sent(owner, k):
            dz(owner).wait_send()
            zs(owner, k).wait_send()

        to_far(sent)

    @pl.when(z > 1)
    def _():
        to_owners(base_z, lambda owner, k: zg_from(k).wait_recv())

    @pl.when(z == 1)
    def _():
        first().wait_recv()

    @pl.when(z == 0)
    def _():
        first().wait_send()
        c2[...] = jnp.zeros_like(c2)

    for e in range(2):
        rows = pl.ds(e * HD, HD)
        at = pl.ds(pl.multiple_of(c * PAIR + e * HD, HD), HD)
        own = loc[at, :]
        before = c2[rows, :].astype(F32)
        even_decay = jnp.where(even, per_row(dl_own, e), per_row(dl_peer, e))
        after = even_decay * before + jnp.where(even, own, loc_recv[rows, :].astype(F32))
        loc_send[rows, :] = jnp.where(even, after, before).astype(BF16)
        here = jnp.where(even, before, after)
        carried[at, :] = here.astype(BF16)
        st_v[at, :] = per_row(dl_own, e) * here + own
    swap_carried = pltpu.make_async_remote_copy(
        loc_send, carried.at[ours], core_s.at[2], core_r.at[2],
        device_id=peer, device_id_type=MESH,
    )
    swap_carried.start()

    def finish(pair):
        for b in range(TOK // BLK):
            rows = pl.ds(b * BLK, BLK)
            for e in range(2):
                at = pl.ds(pl.multiple_of(pair * PAIR + e * HD, HD), HD)
                att = inside[rows, at] + jnp.dot(
                    qs_ref[rows, at], carried[at, :], preferred_element_type=F32
                )
                square = jnp.mean(att * att, axis=-1, keepdims=True)
                out_v[rows, at] = (
                    att * lax.rsqrt(square + 1e-6) * gain[pl.ds(pair * 2 + e, 1), :]
                ).astype(BF16)

    finish(c)
    swap_carried.wait()
    for e in range(2):
        at = pl.ds(pl.multiple_of((1 - c) * PAIR + e * HD, HD), HD)
        decay = jnp.exp(dl_own[pl.ds((1 - c) * 2 + e, 1), :])
        st_v[at, :] = decay * carried[at, :].astype(F32) + loc[at, :]
    finish(1 - c)

    @pl.when(jnp.logical_and(owns, lower))
    def _():
        given(range(2, HZ))
        early().wait_send()

    @pl.when(jnp.logical_and(owns, jnp.logical_not(lower)))
    def _():
        given(range(HZ, NZ))


def local(hidden, base, down, up, decay, gain):
    anyspace = pl.BlockSpec(memory_space=pl.ANY)
    dma = pltpu.SemaphoreType.DMA
    scratch = [
        pltpu.VMEM((TOK, GROUP), BF16),
        pltpu.VMEM((3, TOK, WIDTH), BF16),
        pltpu.VMEM((3 * RANK, GROUP), BF16),
        pltpu.VMEM((3, 3 * RANK, WIDTH), BF16),
        pltpu.VMEM((HEADS, TOK), F32),
        pltpu.VMEM((HEADS, HD), F32),
        pltpu.VMEM((HALF, 2 * RANK), BF16),
        pltpu.VMEM((NTP, LORA_PIECE, 2 * RANK), BF16),
        pltpu.VMEM((HALF, 2 * RANK), BF16),
        pltpu.VMEM((8, TOK), F32),
        pltpu.VMEM((8, TOK), F32),
        pltpu.VMEM((HEADS, TOK, HD), F32),
        pltpu.VMEM((8, HD), F32),
        pltpu.VMEM((8, HD), F32),
        pltpu.VMEM((NZ, 1, HD), F32),
        pltpu.VMEM((NZ, 1, HD), F32),
        pltpu.VMEM((TOK, WIDTH), BF16),
        pltpu.VMEM((TOK, WIDTH), BF16),
        pltpu.VMEM((WIDTH, TOK), BF16),
        pltpu.VMEM((TOK, WIDTH), BF16),
        pltpu.VMEM((TOK, WIDTH), F32),
        pltpu.VMEM((WIDTH, HD), F32),
        pltpu.VMEM((PAIR, HD), BF16),
        pltpu.VMEM((PAIR, HD), BF16),
        pltpu.VMEM((PAIR, HD), BF16),
        pltpu.VMEM((NZ, STATE_PIECE, HD), BF16),
        pltpu.VMEM((HZ, STATE_PIECE, HD), BF16),
        pltpu.VMEM((PAIR, HD), BF16),
        pltpu.VMEM((WIDTH, HD), BF16),
        dma((6,)),
        dma((NTP,)), dma((NTP,)), dma((NTP,)), dma((NTP,)),
        dma((NZ,)), dma((NZ,)), dma((NZ,)), dma((NZ,)), dma((NZ,)), dma((NZ,)),
        dma((4,)), dma((4,)), pltpu.SemaphoreType.REGULAR, pltpu.SemaphoreType.REGULAR,
    ]
    mixed, states = pl.pallas_call(
        kernel,
        out_shape=(
            jax.ShapeDtypeStruct((TOK, WIDTH), BF16),
            jax.ShapeDtypeStruct((WIDTH, HD), F32),
        ),
        in_specs=[anyspace] * 6,
        out_specs=(pl.BlockSpec(memory_space=pltpu.VMEM),) * 2,
        scratch_shapes=scratch,
        compiler_params=pltpu.CompilerParams(
            collective_id=0, has_side_effects=True, vmem_limit_bytes=48 * 1024 * 1024
        ),
        cost_estimate=pl.CostEstimate(
            flops=3_000_000_000, bytes_accessed=6_000_000, transcendentals=6_000_000
        ),
    )(*[pltpu.with_memory_space_constraint(a, pltpu.HBM) for a in (hidden, base, down.T, up, decay.T, gain.reshape(HEADS, HD))])
    return mixed, states.reshape(1, HEADS, HD, HD)


def solution(mesh):
    in_specs = (
        P("ctx", "tp"),
        P(None, "ctx", "tp"),
        P("tp", None),
        P(None, None, "tp"),
        P("ctx", "tp"),
        P("tp"),
    )
    out_specs = (P("ctx", "tp"), P("ctx", "tp", None, None))
    return jax.shard_map(local, mesh=mesh, in_specs=in_specs, out_specs=out_specs, check_vma=False)
```

```python
import jax
import jax.numpy as jnp
from jax import lax
from jax.experimental import pallas as pl
from jax.experimental.pallas import tpu as pltpu
from jax.sharding import PartitionSpec as P

HD = 128
HEADS = 4
TOK = 1024
HALF = 512
RANK = 64
GROUP = 384
WIDTH = HEADS * HD
PAIR = 2 * HD
BLK = 256
NX, NY, NZ = 4, 4, 16
NTP = NX * NY
LORA_PIECE = HALF // NTP
CHUNK = HALF // NX
HZ = NZ // 2
OWNERS = 4
FIRST = 2
EARLY = 7
STATE_PIECE = PAIR // OWNERS
LANES = HD // HEADS
MESH = pl.DeviceIdType.MESH
F32, BF16 = jnp.float32, jnp.bfloat16


def ring(offset, size):
    return min(offset, size - offset)


XY = sorted(range(1, NTP), key=lambda r: -(ring(r // NY, NX) + ring(r % NY, NY)))
ZH = [4, 3, 5, 2, 6, 1, 7]


def order(z):
    return jnp.where(z < HZ, z, jnp.where(z >= 12, 23 - z, z + 4))


CROSS = [*range(FIRST, FIRST + OWNERS), *range(max(EARLY, FIRST + OWNERS), HZ)]
ORDER = [z if z < HZ else (23 - z if z >= 12 else z + 4) for z in range(NZ)]


def silu(v):
    half = 0.5 * v
    return half + half * jnp.tanh(half)


def kernel(
    hid_hbm, base_hbm, dwn_hbm, up_hbm, dec_hbm, gain_hbm,
    out_v, st_v,
    hid, base, dpad, upad, dec, gain, kbase, kup,
    part, rsum, lora,
    cum, wgt, ccol, dl_own, dl_peer, dl_chip, chip_decay,
    q_ref, qs_ref, kt_ref, v_ref, inside,
    loc, loc_send, loc_recv, tot, p1, pre, c2, carried,
    in_sem,
    rs_s, rs_r, ag_s, ag_r, zs_s, zs_r, zg_s, zg_r, dz_s, dz_r, core_s, core_r, near_sem, far_sem,
):
    ctx, tp = lax.axis_index("ctx"), lax.axis_index("tp")
    z, c = ctx // 2, ctx % 2
    x, y = tp // NY, tp % NY
    peer = {"ctx": z * 2 + (1 - c)}

    def plane(r):
        return {"tp": lax.rem(x + r // NY, NX) * NY + lax.rem(y + r % NY, NY)}

    zh = z % HZ
    base_z = z - zh
    lower = z < HZ

    def chip(other):
        return {"ctx": other * 2 + c}

    def along(r):
        return base_z + lax.rem(zh + r, HZ)

    loads = [
        pltpu.make_async_copy(dwn_hbm, dpad.at[pl.ds(RANK, RANK)], in_sem.at[0]),
        pltpu.make_async_copy(hid_hbm, hid, in_sem.at[1]),
        pltpu.make_async_copy(dec_hbm, dec, in_sem.at[2]),
        pltpu.make_async_copy(up_hbm, upad.at[:, pl.ds(RANK, RANK)], in_sem.at[3]),
        pltpu.make_async_copy(base_hbm, base, in_sem.at[4]),
        pltpu.make_async_copy(gain_hbm, gain, in_sem.at[5]),
    ]
    loads[0].start()
    loads[1].start()

    place = order(z)
    barrier = pltpu.get_barrier_semaphore()
    for r in XY:
        pl.semaphore_signal(barrier, inc=1, device_id=plane(r), device_id_type=MESH)
    pl.semaphore_signal(barrier, inc=1, device_id=peer, device_id_type=MESH)
    for load in loads[2:]:
        load.start()
    for k in range(NZ):
        @pl.when(place < ORDER[k])
        def _(k=k):
            pl.semaphore_signal(barrier, inc=1, device_id=chip(k), device_id_type=MESH)

    zeros = jnp.zeros((RANK, GROUP), BF16)
    dpad[pl.ds(0, RANK), :] = zeros
    dpad[pl.ds(2 * RANK, RANK), :] = zeros
    zeros = jnp.zeros((RANK, WIDTH), BF16)
    for i in range(3):
        upad[i, pl.ds(0, RANK), :] = zeros
        upad[i, pl.ds(2 * RANK, RANK), :] = zeros

    loads[0].wait()
    loads[1].wait()
    trans_b = (((1,), (1,)), ((), ()))
    for i in range(2):
        rows = pl.ds(i * BLK, BLK)
        mine = lax.dot_general(
            hid[rows, :], dpad[pl.ds(RANK, 2 * RANK), :], trans_b, preferred_element_type=F32
        ) + lax.dot_general(
            hid[pl.ds(HALF + i * BLK, BLK), :], dpad[pl.ds(0, 2 * RANK), :], trans_b,
            preferred_element_type=F32,
        )
        part[rows, :] = mine.astype(BF16)

    pl.semaphore_wait(barrier, NTP - 1 + 1 + place)

    def rs(r):
        to = plane(r)
        return pltpu.make_async_remote_copy(
            part.at[pl.ds(pl.multiple_of(to["tp"] * LORA_PIECE, LORA_PIECE), LORA_PIECE)],
            rsum.at[r], rs_s.at[r], rs_r.at[r], device_id=to, device_id_type=MESH,
        )

    for r in XY:
        rs(r).start()

    for k in range(NZ):
        same = lower if k < HZ else jnp.logical_not(lower)

        @pl.when(jnp.logical_and(place > ORDER[k], same))
        def _(k=k):
            pl.semaphore_signal(near_sem, inc=1, device_id=chip(k), device_id_type=MESH)

        @pl.when(jnp.logical_and(place > ORDER[k], jnp.logical_and(jnp.logical_not(same), k in CROSS)))
        def _(k=k):
            pl.semaphore_signal(far_sem, inc=1, device_id=chip(k), device_id_type=MESH)

    loads[2].wait()
    run = jnp.concatenate([dec[...], jnp.zeros((8 - HEADS, TOK), F32)], axis=0)
    lane = lax.broadcasted_iota(jnp.int32, (8, TOK), 1)
    step = 1
    while step < TOK:
        run = run + jnp.where(lane >= step, pltpu.roll(run, step, 1), 0.0)
        step *= 2
    last = run[:, TOK - 1 :]
    cum[...] = run
    wgt[...] = jnp.exp(last - run)
    dl_own[...] = jnp.broadcast_to(last, (8, HD))
    swap_decay = pltpu.make_async_remote_copy(
        dl_own, dl_peer, core_s.at[0], core_r.at[0], device_id=peer, device_id_type=MESH
    )
    swap_decay.start()

    loads[3].wait()
    loads[4].wait()

    def turn(i, carry):
        at = pl.ds(pl.multiple_of(i * BLK, BLK), BLK)
        kbase[:, at] = base[1, at, :].T
        return carry

    lax.fori_loop(0, TOK // BLK, turn, 0)
    kup[0] = upad[1, pl.ds(RANK, 2 * RANK), :].T
    kup[1] = upad[1, pl.ds(0, 2 * RANK), :].T

    swap_decay.wait()
    head_of_lane = lax.broadcasted_iota(jnp.int32, (8, HD), 1) // LANES
    dl_chip[z] = jnp.sum(
        jnp.where(
            head_of_lane == lax.broadcasted_iota(jnp.int32, (8, HD), 0),
            dl_own[...] + dl_peer[...], 0.0,
        ),
        axis=0, keepdims=True,
    )

    def dz(owner):
        return pltpu.make_async_remote_copy(
            dl_chip.at[z], dl_chip.at[z], dz_s.at[owner], dz_r.at[z],
            device_id=chip(owner), device_id_type=MESH,
        )

    def dz_from(k):
        return pltpu.make_async_remote_copy(
            dl_chip.at[k], dl_chip.at[k], dz_s.at[0], dz_r.at[k],
            device_id=peer, device_id_type=MESH,
        )

    def to_owners(half, what):
        for k in range(OWNERS):
            owner = half + FIRST + jnp.where(lower, k, OWNERS - 1 - k)

            @pl.when(owner != z)
            def _(owner=owner, k=k):
                what(owner, k)

    mine_at = pl.ds(pl.multiple_of(tp * LORA_PIECE, LORA_PIECE), LORA_PIECE)
    for r in XY:
        rs(r).wait_recv()
    total = part[mine_at, :].astype(F32)
    for r in range(1, NTP):
        total = total + rsum[r].astype(F32)
    lora[mine_at, :] = total.astype(BF16)

    def ag(r):
        return pltpu.make_async_remote_copy(
            lora.at[mine_at], lora.at[mine_at], ag_s.at[r], ag_r.at[r],
            device_id=plane(r), device_id_type=MESH,
        )

    for r in XY:
        ag(r).start()
    for r in XY:
        rs(r).wait_send()
    later = jnp.where(lower, HZ, NZ) - 1 - place

    @pl.when(later > 0)
    def _():
        pl.semaphore_wait(near_sem, later)

    adds = jnp.logical_or(zh < HZ - 1, jnp.logical_and(lower, EARLY == HZ))

    @pl.when(adds)
    def _():
        to_owners(base_z, lambda owner, k: dz(owner).start())

    loads[5].wait()

    def projected(i, a, row, size, lanes):
        return base[i, pl.ds(a * HALF + row, size), lanes].astype(F32) + jnp.dot(
            lora[pl.ds(row, size), :],
            upad[i, pl.ds(RANK - RANK * a, 2 * RANK), lanes],
            preferred_element_type=F32,
        )

    for n, shift in enumerate((0, 1, 3, 2)):
        for ry in range(NY):
            if shift or ry:
                ag(shift * NY + ry).wait_recv()
        row = pl.multiple_of(lax.rem(x + NX - shift, NX) * CHUNK, CHUNK)
        scaled = []
        for a in range(2):
            at = pl.ds(pl.multiple_of(a * HALF + row, CHUNK), CHUNK)
            k = silu(
                kbase[:, at].astype(F32)
                + lax.dot_general(
                    kup[a], lora[pl.ds(row, CHUNK), :], trans_b, preferred_element_type=F32
                )
            ).astype(BF16)
            kt_ref[:, at] = k
            v_ref[at, :] = projected(2, a, row, CHUNK, slice(None)).astype(BF16)
            scaled.append(
                [
                    (k[h * HD : (h + 1) * HD].astype(F32) * wgt[h : h + 1, at]).astype(BF16)
                    for h in range(HEADS)
                ]
            )
        for h in range(HEADS):
            lanes = slice(h * HD, (h + 1) * HD)
            part_sum = sum(
                jnp.dot(
                    scaled[a][h],
                    v_ref[pl.ds(pl.multiple_of(a * HALF + row, CHUNK), CHUNK), lanes],
                    preferred_element_type=F32,
                )
                for a in range(2)
            )
            if n == 0:
                loc[lanes, :] = part_sum
            else:
                loc[lanes, :] += part_sum

    ours = pl.ds(pl.multiple_of(c * PAIR, PAIR), PAIR)
    theirs = pl.ds(pl.multiple_of((1 - c) * PAIR, PAIR), PAIR)
    even = c == 0

    loc_send[...] = loc[theirs, :].astype(BF16)
    swap_local = pltpu.make_async_remote_copy(
        loc_send, loc_recv, core_s.at[1], core_r.at[1], device_id=peer, device_id_type=MESH
    )
    swap_local.start()
    swap_local.wait_recv()

    def per_row(ref, e):
        return jnp.exp(ref[pl.ds(c * 2 + e, 1), :])

    for e in range(2):
        rows = pl.ds(e * HD, HD)
        own = loc[pl.ds(pl.multiple_of(c * PAIR + e * HD, HD), HD), :]
        other = loc_recv[rows, :].astype(F32)
        odd_decay = jnp.where(even, per_row(dl_peer, e), per_row(dl_own, e))
        tot[rows, :] = (
            jnp.where(even, own, other) * odd_decay + jnp.where(even, other, own)
        ).astype(BF16)

    def zs(owner, k):
        return pltpu.make_async_remote_copy(
            tot.at[pl.ds(k * STATE_PIECE, STATE_PIECE)], p1.at[z], zs_s.at[owner], zs_r.at[z],
            device_id=chip(owner), device_id_type=MESH,
        )

    def zs_from(k):
        return pltpu.make_async_remote_copy(
            tot.at[pl.ds(0, STATE_PIECE)], p1.at[k], zs_s.at[0], zs_r.at[k],
            device_id=peer, device_id_type=MESH,
        )

    @pl.when(adds)
    def _():
        to_owners(base_z, lambda owner, k: zs(owner, k).start())

    def first():
        return pltpu.make_async_remote_copy(
            tot, c2, core_s.at[3], core_r.at[3], device_id=chip(1), device_id_type=MESH
        )

    @pl.when(z == 0)
    def _():
        first().start()

    far = jnp.logical_and(lower, z >= EARLY)

    def to_far(what):
        for k in range(OWNERS):
            what(HZ + FIRST + OWNERS - 1 - k, k)

    @pl.when(far)
    def _():
        pl.semaphore_wait(far_sem, HZ)

        def start(owner, k):
            dz(owner).start()
            zs(owner, k).start()

        to_far(start)

    owns = jnp.logical_and(zh >= FIRST, zh < FIRST + OWNERS)
    mine_k = jnp.where(lower, zh - FIRST, FIRST + OWNERS - 1 - zh)
    mine_k = jnp.clip(mine_k, 0, OWNERS - 1)
    piece_at = pl.ds(pl.multiple_of(mine_k * STATE_PIECE, STATE_PIECE), STATE_PIECE)

    def queries(i, carry):
        for a in range(2):
            row = pl.multiple_of(i * BLK, BLK)
            rows = pl.ds(a * HALF + row, BLK)
            q = silu(projected(0, a, row, BLK, slice(None))).astype(BF16)
            q_ref[rows, :] = q
            for h in range(HEADS):
                grow = jnp.exp(ccol[h, rows, :])
                qs_ref[rows, h * HD : (h + 1) * HD] = (
                    q[:, h * HD : (h + 1) * HD].astype(F32) * grow
                ).astype(BF16)
        return carry

    tri = lax.broadcasted_iota(jnp.int32, (BLK, BLK), 0) >= lax.broadcasted_iota(
        jnp.int32, (BLK, BLK), 1
    )

    def attend(h, carry):
        at = pl.ds(pl.multiple_of(h * HD, HD), HD)
        for b in range(TOK // BLK):
            rows = pl.ds(b * BLK, BLK)
            q = q_ref[rows, at]
            col = ccol[h, rows, :]
            col = jnp.concatenate([col, col], axis=1)
            acc = jnp.zeros((BLK, HD), F32)
            for s in range(b + 1):
                cols = pl.ds(s * BLK, BLK)
                spread = col - cum[pl.ds(h, 1), cols]
                if s == b:
                    spread = jnp.where(tri, spread, -1e30)
                score = jnp.dot(q, kt_ref[at, cols], preferred_element_type=F32)
                weight = (jnp.exp(spread) * score).astype(BF16)
                acc = acc + jnp.dot(weight, v_ref[cols, at], preferred_element_type=F32)
            inside[rows, at] = acc
        return carry

    heads_before = jnp.where(jnp.logical_or(z == 4, z == 5), 1, 2)
    def ccol_of(h, carry):
        ccol[h] = jnp.broadcast_to(cum[pl.ds(h, 1), :], (HD, TOK)).T
        return carry

    lax.fori_loop(0, HEADS, ccol_of, 0)
    lax.fori_loop(0, HALF // BLK, queries, 0)
    lax.fori_loop(0, heads_before, attend, 0)

    head_lane = (c * 2 + mine_k // 2) * LANES
    lane_of = lax.broadcasted_iota(jnp.int32, (1, 1, HD), 2)

    def arrive(k):
        @pl.when(z != k)
        def _():
            zs_from(k).wait_recv()

    def decays(first, last):
        for k in range(first, last):
            @pl.when(z != k)
            def _(k=k):
                dz_from(k).wait_recv()

        log = jnp.sum(
            jnp.where(lane_of == head_lane, dl_chip[first:last], 0.0), axis=2, keepdims=True
        )
        chip_decay[first:last] = jnp.broadcast_to(jnp.exp(log), (last - first, 1, HD))

    def advance(state, k):
        return chip_decay[k] * state + p1[k].astype(F32)

    def zg(b):
        return pltpu.make_async_remote_copy(
            pre.at[b % HZ], c2.at[piece_at], zg_s.at[b % HZ], zg_r.at[mine_k],
            device_id=chip(b), device_id_type=MESH,
        )

    def zg_from(k):
        rows = pl.ds(k * STATE_PIECE, STATE_PIECE)
        return pltpu.make_async_remote_copy(
            pre.at[0], c2.at[rows], zg_s.at[0], zg_r.at[k], device_id=peer, device_id_type=MESH
        )

    def give(b):
        @pl.when(z != b)
        def _():
            zg(b).start()

    def given(blocks):
        for b in blocks:
            @pl.when(z != b)
            def _(b=b):
                zg(b).wait_send()

    def early():
        return pltpu.make_async_remote_copy(
            pre.at[EARLY % HZ], p1.at[EARLY - 1], zs_s.at[0], zs_r.at[EARLY - 1],
            device_id=chip(NZ - 1 - z), device_id_type=MESH,
        )

    @pl.when(jnp.logical_and(owns, lower))
    def _():
        p1[z] = tot[piece_at, :]
        ends = max(HZ - 1, EARLY)
        decays(0, ends)
        state = jnp.zeros((STATE_PIECE, HD), F32)
        for k in range(ends):
            arrive(k)
            state = advance(state, k)
            pre[(k + 1) % HZ] = state.astype(BF16)
            if k == EARLY - 1:
                @pl.when(jnp.logical_not(far))
                def _():
                    pl.semaphore_wait(far_sem, HZ)

                early().start()
            if 1 < k + 1 < HZ:
                give(k + 1)

    @pl.when(jnp.logical_and(owns, jnp.logical_not(lower)))
    def _():
        p1[z] = tot[piece_at, :]
        decays(EARLY, NZ - 1)
        zs_from(EARLY - 1).wait_recv()
        state = p1[EARLY - 1].astype(F32)
        for k in range(EARLY, NZ - 1):
            arrive(k)
            state = advance(state, k)
            if k >= HZ - 1:
                pre[k + 1 - HZ] = state.astype(BF16)
        for b in (15, 8, 14, 9, 13, 12, 10, 11):
            give(b)

    @pl.when(owns)
    def _():
        c2[piece_at, :] = pre[zh]

    lax.fori_loop(heads_before, HEADS, attend, 0)
    for r in XY:
        ag(r).wait_send()

    swap_local.wait_send()

    @pl.when(adds)
    def _():
        to_owners(base_z, lambda owner, k: dz(owner).wait_send())
        to_owners(base_z, lambda owner, k: zs(owner, k).wait_send())

    @pl.when(far)
    def _():
        def sent(owner, k):
            dz(owner).wait_send()
            zs(owner, k).wait_send()

        to_far(sent)

    @pl.when(z > 1)
    def _():
        to_owners(base_z, lambda owner, k: zg_from(k).wait_recv())

    @pl.when(z == 1)
    def _():
        first().wait_recv()

    @pl.when(z == 0)
    def _():
        first().wait_send()
        c2[...] = jnp.zeros_like(c2)

    states = []
    for e in range(2):
        rows = pl.ds(e * HD, HD)
        own = loc[pl.ds(pl.multiple_of(c * PAIR + e * HD, HD), HD), :]
        before = c2[rows, :].astype(F32)
        even_decay = jnp.where(even, per_row(dl_own, e), per_row(dl_peer, e))
        after = even_decay * before + jnp.where(even, own, loc_recv[rows, :].astype(F32))
        loc_send[rows, :] = jnp.where(even, after, before).astype(BF16)
        states.append((own, jnp.where(even, before, after)))
    swap_carried = pltpu.make_async_remote_copy(
        loc_send, carried.at[ours], core_s.at[2], core_r.at[2],
        device_id=peer, device_id_type=MESH,
    )
    swap_carried.start()
    for e, (own, here) in enumerate(states):
        at = pl.ds(pl.multiple_of(c * PAIR + e * HD, HD), HD)
        carried[at, :] = here.astype(BF16)
        st_v[at, :] = per_row(dl_own, e) * here + own

    def finish(pair):
        for b in range(TOK // BLK):
            rows = pl.ds(b * BLK, BLK)
            for e in range(2):
                at = pl.ds(pl.multiple_of(pair * PAIR + e * HD, HD), HD)
                att = inside[rows, at] + jnp.dot(
                    qs_ref[rows, at], carried[at, :], preferred_element_type=F32
                )
                square = jnp.mean(att * att, axis=-1, keepdims=True)
                out_v[rows, at] = (
                    att * lax.rsqrt(square + 1e-6) * gain[pl.ds(pair * 2 + e, 1), :]
                ).astype(BF16)

    finish(c)
    swap_carried.wait_recv()
    for e in range(2):
        at = pl.ds(pl.multiple_of((1 - c) * PAIR + e * HD, HD), HD)
        decay = jnp.exp(dl_own[pl.ds((1 - c) * 2 + e, 1), :])
        st_v[at, :] = decay * carried[at, :].astype(F32) + loc[at, :]
    finish(1 - c)

    swap_carried.wait_send()

    @pl.when(jnp.logical_and(owns, lower))
    def _():
        given(range(2, HZ))
        early().wait_send()

    @pl.when(jnp.logical_and(owns, jnp.logical_not(lower)))
    def _():
        given(range(HZ, NZ))


def local(hidden, base, down, up, decay, gain):
    anyspace = pl.BlockSpec(memory_space=pl.ANY)
    dma = pltpu.SemaphoreType.DMA
    scratch = [
        pltpu.VMEM((TOK, GROUP), BF16),
        pltpu.VMEM((3, TOK, WIDTH), BF16),
        pltpu.VMEM((3 * RANK, GROUP), BF16),
        pltpu.VMEM((3, 3 * RANK, WIDTH), BF16),
        pltpu.VMEM((HEADS, TOK), F32),
        pltpu.VMEM((HEADS, HD), F32),
        pltpu.VMEM((WIDTH, TOK), BF16),
        pltpu.VMEM((2, WIDTH, 2 * RANK), BF16),
        pltpu.VMEM((HALF, 2 * RANK), BF16),
        pltpu.VMEM((NTP, LORA_PIECE, 2 * RANK), BF16),
        pltpu.VMEM((HALF, 2 * RANK), BF16),
        pltpu.VMEM((8, TOK), F32),
        pltpu.VMEM((8, TOK), F32),
        pltpu.VMEM((HEADS, TOK, HD), F32),
        pltpu.VMEM((8, HD), F32),
        pltpu.VMEM((8, HD), F32),
        pltpu.VMEM((NZ, 1, HD), F32),
        pltpu.VMEM((NZ, 1, HD), F32),
        pltpu.VMEM((TOK, WIDTH), BF16),
        pltpu.VMEM((TOK, WIDTH), BF16),
        pltpu.VMEM((WIDTH, TOK), BF16),
        pltpu.VMEM((TOK, WIDTH), BF16),
        pltpu.VMEM((TOK, WIDTH), F32),
        pltpu.VMEM((WIDTH, HD), F32),
        pltpu.VMEM((PAIR, HD), BF16),
        pltpu.VMEM((PAIR, HD), BF16),
        pltpu.VMEM((PAIR, HD), BF16),
        pltpu.VMEM((NZ, STATE_PIECE, HD), BF16),
        pltpu.VMEM((HZ, STATE_PIECE, HD), BF16),
        pltpu.VMEM((PAIR, HD), BF16),
        pltpu.VMEM((WIDTH, HD), BF16),
        dma((6,)),
        dma((NTP,)), dma((NTP,)), dma((NTP,)), dma((NTP,)),
        dma((NZ,)), dma((NZ,)), dma((NZ,)), dma((NZ,)), dma((NZ,)), dma((NZ,)),
        dma((4,)), dma((4,)), pltpu.SemaphoreType.REGULAR, pltpu.SemaphoreType.REGULAR,
    ]
    mixed, states = pl.pallas_call(
        kernel,
        out_shape=(
            jax.ShapeDtypeStruct((TOK, WIDTH), BF16),
            jax.ShapeDtypeStruct((WIDTH, HD), F32),
        ),
        in_specs=[anyspace] * 6,
        out_specs=(pl.BlockSpec(memory_space=pltpu.VMEM),) * 2,
        scratch_shapes=scratch,
        compiler_params=pltpu.CompilerParams(
            collective_id=0, has_side_effects=True, vmem_limit_bytes=48 * 1024 * 1024
        ),
        cost_estimate=pl.CostEstimate(
            flops=3_000_000_000, bytes_accessed=6_000_000, transcendentals=6_000_000
        ),
    )(*[pltpu.with_memory_space_constraint(a, pltpu.HBM) for a in (hidden, base, down.T, up, decay.T, gain.reshape(HEADS, HD))])
    return mixed, states.reshape(1, HEADS, HD, HD)


def solution(mesh):
    in_specs = (
        P("ctx", "tp"),
        P(None, "ctx", "tp"),
        P("tp", None),
        P(None, None, "tp"),
        P("ctx", "tp"),
        P("tp"),
    )
    out_specs = (P("ctx", "tp"), P("ctx", "tp", None, None))
    return jax.shard_map(local, mesh=mesh, in_specs=in_specs, out_specs=out_specs, check_vma=False)
```

```python
import jax
import jax.numpy as jnp
from jax import lax
from jax.experimental import pallas as pl
from jax.experimental.pallas import tpu as pltpu
from jax.sharding import PartitionSpec as P

HD = 128
HEADS = 4
TOK = 1024
HALF = 512
RANK = 64
GROUP = 384
WIDTH = HEADS * HD
PAIR = 2 * HD
BLK = 256
NX, NY, NZ = 4, 4, 16
NTP = NX * NY
LORA_PIECE = HALF // NTP
CHUNK = HALF // NX
HZ = NZ // 2
OWNERS = 4
LOWER = (2, 3, 4, 5)
UPPER = (13, 12, 10, 9)
EARLY = 7
STATE_PIECE = PAIR // OWNERS
LANES = HD // HEADS
MESH = pl.DeviceIdType.MESH
F32, BF16 = jnp.float32, jnp.bfloat16


def ring(offset, size):
    return min(offset, size - offset)


XY = sorted(range(1, NTP), key=lambda r: -(ring(r // NY, NX) + ring(r % NY, NY)))
ZH = [4, 3, 5, 2, 6, 1, 7]


def order(z):
    return jnp.where(z < HZ, z, jnp.where(z >= 12, 23 - z, z + 4))


CROSS = sorted({*LOWER, *range(EARLY, HZ)})
ORDER = [z if z < HZ else (23 - z if z >= 12 else z + 4) for z in range(NZ)]


def silu(v):
    half = 0.5 * v
    return half + half * jnp.tanh(half)


def kernel(
    hid_hbm, base_hbm, dwn_hbm, up_hbm, dec_hbm, gain_hbm,
    out_v, st_v,
    hid, base, dpad, upad, dec, gain, kbase, kup,
    part, rsum, lora,
    cum, wgt, ccol, dl_own, dl_peer, dl_chip, chip_decay,
    q_ref, qs_ref, kt_ref, v_ref, inside,
    loc, loc_send, loc_recv, tot, p1, pre, later_part, c2, carried,
    in_sem,
    rs_s, rs_r, ag_s, ag_r, zs_s, zs_r, zg_s, zg_r, dz_s, dz_r, core_s, core_r, near_sem, far_sem,
):
    ctx, tp = lax.axis_index("ctx"), lax.axis_index("tp")
    z, c = ctx // 2, ctx % 2
    x, y = tp // NY, tp % NY
    peer = {"ctx": z * 2 + (1 - c)}

    def plane(r):
        return {"tp": lax.rem(x + r // NY, NX) * NY + lax.rem(y + r % NY, NY)}

    zh = z % HZ
    base_z = z - zh
    lower = z < HZ

    def chip(other):
        return {"ctx": other * 2 + c}

    def along(r):
        return base_z + lax.rem(zh + r, HZ)

    loads = [
        pltpu.make_async_copy(dwn_hbm, dpad.at[pl.ds(RANK, RANK)], in_sem.at[0]),
        pltpu.make_async_copy(hid_hbm, hid, in_sem.at[1]),
        pltpu.make_async_copy(dec_hbm, dec, in_sem.at[2]),
        pltpu.make_async_copy(up_hbm, upad.at[:, pl.ds(RANK, RANK)], in_sem.at[3]),
        pltpu.make_async_copy(base_hbm, base, in_sem.at[4]),
        pltpu.make_async_copy(gain_hbm, gain, in_sem.at[5]),
    ]
    loads[0].start()
    loads[1].start()

    place = order(z)
    barrier = pltpu.get_barrier_semaphore()
    for r in XY:
        pl.semaphore_signal(barrier, inc=1, device_id=plane(r), device_id_type=MESH)
    pl.semaphore_signal(barrier, inc=1, device_id=peer, device_id_type=MESH)
    for load in loads[2:]:
        load.start()
    for k in range(NZ):
        @pl.when(place < ORDER[k])
        def _(k=k):
            pl.semaphore_signal(barrier, inc=1, device_id=chip(k), device_id_type=MESH)

    zeros = jnp.zeros((RANK, GROUP), BF16)
    dpad[pl.ds(0, RANK), :] = zeros
    dpad[pl.ds(2 * RANK, RANK), :] = zeros
    zeros = jnp.zeros((RANK, WIDTH), BF16)
    for i in range(3):
        upad[i, pl.ds(0, RANK), :] = zeros
        upad[i, pl.ds(2 * RANK, RANK), :] = zeros

    loads[0].wait()
    loads[1].wait()
    trans_b = (((1,), (1,)), ((), ()))
    for i in range(2):
        rows = pl.ds(i * BLK, BLK)
        mine = lax.dot_general(
            hid[rows, :], dpad[pl.ds(RANK, 2 * RANK), :], trans_b, preferred_element_type=F32
        ) + lax.dot_general(
            hid[pl.ds(HALF + i * BLK, BLK), :], dpad[pl.ds(0, 2 * RANK), :], trans_b,
            preferred_element_type=F32,
        )
        part[rows, :] = mine.astype(BF16)

    pl.semaphore_wait(barrier, NTP - 1 + 1 + place)

    def rs(r):
        to = plane(r)
        return pltpu.make_async_remote_copy(
            part.at[pl.ds(pl.multiple_of(to["tp"] * LORA_PIECE, LORA_PIECE), LORA_PIECE)],
            rsum.at[r], rs_s.at[r], rs_r.at[r], device_id=to, device_id_type=MESH,
        )

    for r in XY:
        rs(r).start()

    for k in range(NZ):
        same = lower if k < HZ else jnp.logical_not(lower)

        @pl.when(jnp.logical_and(place > ORDER[k], same))
        def _(k=k):
            pl.semaphore_signal(near_sem, inc=1, device_id=chip(k), device_id_type=MESH)

        @pl.when(jnp.logical_and(place > ORDER[k], jnp.logical_and(jnp.logical_not(same), k in CROSS)))
        def _(k=k):
            pl.semaphore_signal(far_sem, inc=1, device_id=chip(k), device_id_type=MESH)

    loads[2].wait()
    run = jnp.concatenate([dec[...], jnp.zeros((8 - HEADS, TOK), F32)], axis=0)
    lane = lax.broadcasted_iota(jnp.int32, (8, TOK), 1)
    step = 1
    while step < TOK:
        run = run + jnp.where(lane >= step, pltpu.roll(run, step, 1), 0.0)
        step *= 2
    last = run[:, TOK - 1 :]
    cum[...] = run
    wgt[...] = jnp.exp(last - run)
    dl_own[...] = jnp.broadcast_to(last, (8, HD))
    swap_decay = pltpu.make_async_remote_copy(
        dl_own, dl_peer, core_s.at[0], core_r.at[0], device_id=peer, device_id_type=MESH
    )
    swap_decay.start()

    loads[3].wait()
    loads[4].wait()

    def turn(i, carry):
        at = pl.ds(pl.multiple_of(i * BLK, BLK), BLK)
        kbase[:, at] = base[1, at, :].T
        return carry

    lax.fori_loop(0, TOK // BLK, turn, 0)
    kup[0] = upad[1, pl.ds(RANK, 2 * RANK), :].T
    kup[1] = upad[1, pl.ds(0, 2 * RANK), :].T

    swap_decay.wait()
    head_of_lane = lax.broadcasted_iota(jnp.int32, (8, HD), 1) // LANES
    dl_chip[z] = jnp.sum(
        jnp.where(
            head_of_lane == lax.broadcasted_iota(jnp.int32, (8, HD), 0),
            dl_own[...] + dl_peer[...], 0.0,
        ),
        axis=0, keepdims=True,
    )

    def dz(owner):
        return pltpu.make_async_remote_copy(
            dl_chip.at[z], dl_chip.at[z], dz_s.at[owner], dz_r.at[z],
            device_id=chip(owner), device_id_type=MESH,
        )

    def dz_from(k):
        return pltpu.make_async_remote_copy(
            dl_chip.at[k], dl_chip.at[k], dz_s.at[0], dz_r.at[k],
            device_id=peer, device_id_type=MESH,
        )

    def to_owners(what):
        for k in range(OWNERS):
            owner = jnp.where(lower, LOWER[k], UPPER[k])

            @pl.when(owner != z)
            def _(owner=owner, k=k):
                what(owner, k)

    mine_at = pl.ds(pl.multiple_of(tp * LORA_PIECE, LORA_PIECE), LORA_PIECE)
    for r in XY:
        rs(r).wait_recv()
    total = part[mine_at, :].astype(F32)
    for r in range(1, NTP):
        total = total + rsum[r].astype(F32)
    lora[mine_at, :] = total.astype(BF16)

    def ag(r):
        return pltpu.make_async_remote_copy(
            lora.at[mine_at], lora.at[mine_at], ag_s.at[r], ag_r.at[r],
            device_id=plane(r), device_id_type=MESH,
        )

    for r in XY:
        ag(r).start()
    for r in XY:
        rs(r).wait_send()
    later = jnp.where(lower, HZ, NZ) - 1 - place

    @pl.when(later > 0)
    def _():
        pl.semaphore_wait(near_sem, later)

    adds = jnp.logical_or(zh < HZ - 1, jnp.logical_and(lower, EARLY == HZ))

    @pl.when(adds)
    def _():
        to_owners(lambda owner, k: dz(owner).start())

    loads[5].wait()

    def projected(i, a, row, size, lanes):
        return base[i, pl.ds(a * HALF + row, size), lanes].astype(F32) + jnp.dot(
            lora[pl.ds(row, size), :],
            upad[i, pl.ds(RANK - RANK * a, 2 * RANK), lanes],
            preferred_element_type=F32,
        )

    for n, shift in enumerate((0, 1, 3, 2)):
        for ry in range(NY):
            if shift or ry:
                ag(shift * NY + ry).wait_recv()
        row = pl.multiple_of(lax.rem(x + NX - shift, NX) * CHUNK, CHUNK)
        scaled = []
        for a in range(2):
            at = pl.ds(pl.multiple_of(a * HALF + row, CHUNK), CHUNK)
            k = silu(
                kbase[:, at].astype(F32)
                + lax.dot_general(
                    kup[a], lora[pl.ds(row, CHUNK), :], trans_b, preferred_element_type=F32
                )
            ).astype(BF16)
            kt_ref[:, at] = k
            v_ref[at, :] = projected(2, a, row, CHUNK, slice(None)).astype(BF16)
            scaled.append(
                [
                    (k[h * HD : (h + 1) * HD].astype(F32) * wgt[h : h + 1, at]).astype(BF16)
                    for h in range(HEADS)
                ]
            )
        for h in range(HEADS):
            lanes = slice(h * HD, (h + 1) * HD)
            part_sum = sum(
                jnp.dot(
                    scaled[a][h],
                    v_ref[pl.ds(pl.multiple_of(a * HALF + row, CHUNK), CHUNK), lanes],
                    preferred_element_type=F32,
                )
                for a in range(2)
            )
            if n == 0:
                loc[lanes, :] = part_sum
            else:
                loc[lanes, :] += part_sum

    ours = pl.ds(pl.multiple_of(c * PAIR, PAIR), PAIR)
    theirs = pl.ds(pl.multiple_of((1 - c) * PAIR, PAIR), PAIR)
    even = c == 0

    loc_send[...] = loc[theirs, :].astype(BF16)
    swap_local = pltpu.make_async_remote_copy(
        loc_send, loc_recv, core_s.at[1], core_r.at[1], device_id=peer, device_id_type=MESH
    )
    swap_local.start()
    swap_local.wait_recv()

    def per_row(ref, e):
        return jnp.exp(ref[pl.ds(c * 2 + e, 1), :])

    for e in range(2):
        rows = pl.ds(e * HD, HD)
        own = loc[pl.ds(pl.multiple_of(c * PAIR + e * HD, HD), HD), :]
        other = loc_recv[rows, :].astype(F32)
        odd_decay = jnp.where(even, per_row(dl_peer, e), per_row(dl_own, e))
        tot[rows, :] = (
            jnp.where(even, own, other) * odd_decay + jnp.where(even, other, own)
        ).astype(BF16)

    def zs(owner, k):
        return pltpu.make_async_remote_copy(
            tot.at[pl.ds(k * STATE_PIECE, STATE_PIECE)], p1.at[z], zs_s.at[owner], zs_r.at[z],
            device_id=chip(owner), device_id_type=MESH,
        )

    def zs_from(k):
        return pltpu.make_async_remote_copy(
            tot.at[pl.ds(0, STATE_PIECE)], p1.at[k], zs_s.at[0], zs_r.at[k],
            device_id=peer, device_id_type=MESH,
        )

    @pl.when(adds)
    def _():
        to_owners(lambda owner, k: zs(owner, k).start())

    def first():
        return pltpu.make_async_remote_copy(
            tot, c2, core_s.at[3], core_r.at[3], device_id=chip(1), device_id_type=MESH
        )

    @pl.when(z == 0)
    def _():
        first().start()

    far = jnp.logical_and(lower, z >= EARLY)

    def to_far(what):
        for k in range(OWNERS):
            what(UPPER[k], k)

    @pl.when(far)
    def _():
        pl.semaphore_wait(far_sem, HZ)

        def start(owner, k):
            dz(owner).start()
            zs(owner, k).start()

        to_far(start)

    mine_k, partner, owns = 0, 0, z < 0
    for k in range(OWNERS):
        here = jnp.logical_or(z == LOWER[k], z == UPPER[k])
        mine_k = jnp.where(here, k, mine_k)
        partner = jnp.where(here, UPPER[k], partner)
        owns = jnp.logical_or(owns, here)
    piece_at = pl.ds(pl.multiple_of(mine_k * STATE_PIECE, STATE_PIECE), STATE_PIECE)

    def queries(i, carry):
        for a in range(2):
            row = pl.multiple_of(i * BLK, BLK)
            rows = pl.ds(a * HALF + row, BLK)
            q = silu(projected(0, a, row, BLK, slice(None))).astype(BF16)
            q_ref[rows, :] = q
            for h in range(HEADS):
                grow = jnp.exp(ccol[h, rows, :])
                qs_ref[rows, h * HD : (h + 1) * HD] = (
                    q[:, h * HD : (h + 1) * HD].astype(F32) * grow
                ).astype(BF16)
        return carry

    tri = lax.broadcasted_iota(jnp.int32, (BLK, BLK), 0) >= lax.broadcasted_iota(
        jnp.int32, (BLK, BLK), 1
    )

    def attend(h, carry):
        at = pl.ds(pl.multiple_of(h * HD, HD), HD)
        for b in range(TOK // BLK):
            rows = pl.ds(b * BLK, BLK)
            q = q_ref[rows, at]
            col = ccol[h, rows, :]
            col = jnp.concatenate([col, col], axis=1)
            acc = jnp.zeros((BLK, HD), F32)
            for s in range(b + 1):
                cols = pl.ds(s * BLK, BLK)
                spread = col - cum[pl.ds(h, 1), cols]
                if s == b:
                    spread = jnp.where(tri, spread, -1e30)
                score = jnp.dot(q, kt_ref[at, cols], preferred_element_type=F32)
                weight = (jnp.exp(spread) * score).astype(BF16)
                acc = acc + jnp.dot(weight, v_ref[cols, at], preferred_element_type=F32)
            inside[rows, at] = acc
        return carry

    heads_before = jnp.where(z >= 4, 1, 2)
    def ccol_of(h, carry):
        ccol[h] = jnp.broadcast_to(cum[pl.ds(h, 1), :], (HD, TOK)).T
        return carry

    lax.fori_loop(0, HEADS, ccol_of, 0)
    lax.fori_loop(0, HALF // BLK, queries, 0)
    lax.fori_loop(0, heads_before, attend, 0)

    head_lane = (c * 2 + mine_k // 2) * LANES
    lane_of = lax.broadcasted_iota(jnp.int32, (1, 1, HD), 2)

    def arrive(k):
        @pl.when(z != k)
        def _():
            zs_from(k).wait_recv()

    def decays(first, last):
        for k in range(first, last):
            @pl.when(z != k)
            def _(k=k):
                dz_from(k).wait_recv()

        log = jnp.sum(
            jnp.where(lane_of == head_lane, dl_chip[first:last], 0.0), axis=2, keepdims=True
        )
        chip_decay[first:last] = jnp.broadcast_to(jnp.exp(log), (last - first, 1, HD))

    def advance(state, k):
        return chip_decay[k] * state + p1[k].astype(F32)

    def zg(b):
        return pltpu.make_async_remote_copy(
            pre.at[b % HZ], c2.at[piece_at], zg_s.at[b % HZ], zg_r.at[mine_k],
            device_id=chip(b), device_id_type=MESH,
        )

    def zg_from(k):
        rows = pl.ds(k * STATE_PIECE, STATE_PIECE)
        return pltpu.make_async_remote_copy(
            pre.at[0], c2.at[rows], zg_s.at[0], zg_r.at[k], device_id=peer, device_id_type=MESH
        )

    def give(b):
        @pl.when(z != b)
        def _():
            zg(b).start()

    def given(blocks):
        for b in blocks:
            @pl.when(z != b)
            def _(b=b):
                zg(b).wait_send()

    def early():
        return pltpu.make_async_remote_copy(
            pre.at[EARLY % HZ], p1.at[EARLY - 1], zs_s.at[0], zs_r.at[EARLY - 1],
            device_id=chip(partner), device_id_type=MESH,
        )

    @pl.when(jnp.logical_and(owns, lower))
    def _():
        p1[z] = tot[piece_at, :]
        ends = max(HZ - 1, EARLY)
        decays(0, ends)
        state = jnp.zeros((STATE_PIECE, HD), F32)
        for k in range(ends):
            arrive(k)
            state = advance(state, k)
            pre[(k + 1) % HZ] = state.astype(BF16)
            if k == EARLY - 1:
                @pl.when(jnp.logical_not(far))
                def _():
                    pl.semaphore_wait(far_sem, HZ)

                early().start()
            if 1 < k + 1 < HZ:
                give(k + 1)

    @pl.when(jnp.logical_and(owns, jnp.logical_not(lower)))
    def _():
        p1[z] = tot[piece_at, :]
        decays(EARLY, NZ - 1)
        state = jnp.zeros((STATE_PIECE, HD), F32)
        grow = jnp.ones((1, HD), F32)
        grown = {}
        for k in range(EARLY, NZ - 1):
            arrive(k)
            state = advance(state, k)
            grow = grow * chip_decay[k]
            if k >= HZ - 1:
                later_part[k + 1 - HZ] = state
                grown[k + 1] = grow
        zs_from(EARLY - 1).wait_recv()
        start = p1[EARLY - 1].astype(F32)
        for b in (15, 8, 14, 9, 13, 12, 10, 11):
            pre[b - HZ] = (grown[b] * start + later_part[b - HZ]).astype(BF16)
            give(b)

    @pl.when(owns)
    def _():
        c2[piece_at, :] = pre[zh]

    lax.fori_loop(heads_before, HEADS, attend, 0)
    for r in XY:
        ag(r).wait_send()

    swap_local.wait_send()

    @pl.when(adds)
    def _():
        to_owners(lambda owner, k: dz(owner).wait_send())
        to_owners(lambda owner, k: zs(owner, k).wait_send())

    @pl.when(far)
    def _():
        def sent(owner, k):
            dz(owner).wait_send()
            zs(owner, k).wait_send()

        to_far(sent)

    @pl.when(z > 1)
    def _():
        to_owners(lambda owner, k: zg_from(k).wait_recv())

    @pl.when(z == 1)
    def _():
        first().wait_recv()

    @pl.when(z == 0)
    def _():
        first().wait_send()
        c2[...] = jnp.zeros_like(c2)

    states = []
    for e in range(2):
        rows = pl.ds(e * HD, HD)
        own = loc[pl.ds(pl.multiple_of(c * PAIR + e * HD, HD), HD), :]
        before = c2[rows, :].astype(F32)
        even_decay = jnp.where(even, per_row(dl_own, e), per_row(dl_peer, e))
        after = even_decay * before + jnp.where(even, own, loc_recv[rows, :].astype(F32))
        loc_send[rows, :] = jnp.where(even, after, before).astype(BF16)
        states.append((own, jnp.where(even, before, after)))
    swap_carried = pltpu.make_async_remote_copy(
        loc_send, carried.at[ours], core_s.at[2], core_r.at[2],
        device_id=peer, device_id_type=MESH,
    )
    swap_carried.start()
    for e, (own, here) in enumerate(states):
        at = pl.ds(pl.multiple_of(c * PAIR + e * HD, HD), HD)
        carried[at, :] = here.astype(BF16)
        st_v[at, :] = per_row(dl_own, e) * here + own

    def finish(i, carry):
        pair = jnp.where(i == 0, c, 1 - c)

        @pl.when(i == 1)
        def _():
            swap_carried.wait_recv()
            for e in range(2):
                at = pl.ds(pl.multiple_of((1 - c) * PAIR + e * HD, HD), HD)
                decay = jnp.exp(dl_own[pl.ds((1 - c) * 2 + e, 1), :])
                st_v[at, :] = decay * carried[at, :].astype(F32) + loc[at, :]

        for b in range(TOK // BLK):
            rows = pl.ds(b * BLK, BLK)
            for e in range(2):
                at = pl.ds(pl.multiple_of(pair * PAIR + e * HD, HD), HD)
                att = inside[rows, at] + jnp.dot(
                    qs_ref[rows, at], carried[at, :], preferred_element_type=F32
                )
                square = jnp.mean(att * att, axis=-1, keepdims=True)
                out_v[rows, at] = (
                    att * lax.rsqrt(square + 1e-6) * gain[pl.ds(pair * 2 + e, 1), :]
                ).astype(BF16)
        return carry

    lax.fori_loop(0, 2, finish, 0)
    swap_carried.wait_send()

    @pl.when(jnp.logical_and(owns, lower))
    def _():
        given(range(2, HZ))
        early().wait_send()

    @pl.when(jnp.logical_and(owns, jnp.logical_not(lower)))
    def _():
        given(range(HZ, NZ))


def local(hidden, base, down, up, decay, gain):
    anyspace = pl.BlockSpec(memory_space=pl.ANY)
    dma = pltpu.SemaphoreType.DMA
    scratch = [
        pltpu.VMEM((TOK, GROUP), BF16),
        pltpu.VMEM((3, TOK, WIDTH), BF16),
        pltpu.VMEM((3 * RANK, GROUP), BF16),
        pltpu.VMEM((3, 3 * RANK, WIDTH), BF16),
        pltpu.VMEM((HEADS, TOK), F32),
        pltpu.VMEM((HEADS, HD), F32),
        pltpu.VMEM((WIDTH, TOK), BF16),
        pltpu.VMEM((2, WIDTH, 2 * RANK), BF16),
        pltpu.VMEM((HALF, 2 * RANK), BF16),
        pltpu.VMEM((NTP, LORA_PIECE, 2 * RANK), BF16),
        pltpu.VMEM((HALF, 2 * RANK), BF16),
        pltpu.VMEM((8, TOK), F32),
        pltpu.VMEM((8, TOK), F32),
        pltpu.VMEM((HEADS, TOK, HD), F32),
        pltpu.VMEM((8, HD), F32),
        pltpu.VMEM((8, HD), F32),
        pltpu.VMEM((NZ, 1, HD), F32),
        pltpu.VMEM((NZ, 1, HD), F32),
        pltpu.VMEM((TOK, WIDTH), BF16),
        pltpu.VMEM((TOK, WIDTH), BF16),
        pltpu.VMEM((WIDTH, TOK), BF16),
        pltpu.VMEM((TOK, WIDTH), BF16),
        pltpu.VMEM((TOK, WIDTH), F32),
        pltpu.VMEM((WIDTH, HD), F32),
        pltpu.VMEM((PAIR, HD), BF16),
        pltpu.VMEM((PAIR, HD), BF16),
        pltpu.VMEM((PAIR, HD), BF16),
        pltpu.VMEM((NZ, STATE_PIECE, HD), BF16),
        pltpu.VMEM((HZ, STATE_PIECE, HD), BF16),
        pltpu.VMEM((HZ, STATE_PIECE, HD), F32),
        pltpu.VMEM((PAIR, HD), BF16),
        pltpu.VMEM((WIDTH, HD), BF16),
        dma((6,)),
        dma((NTP,)), dma((NTP,)), dma((NTP,)), dma((NTP,)),
        dma((NZ,)), dma((NZ,)), dma((NZ,)), dma((NZ,)), dma((NZ,)), dma((NZ,)),
        dma((4,)), dma((4,)), pltpu.SemaphoreType.REGULAR, pltpu.SemaphoreType.REGULAR,
    ]
    mixed, states = pl.pallas_call(
        kernel,
        out_shape=(
            jax.ShapeDtypeStruct((TOK, WIDTH), BF16),
            jax.ShapeDtypeStruct((WIDTH, HD), F32),
        ),
        in_specs=[anyspace] * 6,
        out_specs=(pl.BlockSpec(memory_space=pltpu.VMEM),) * 2,
        scratch_shapes=scratch,
        compiler_params=pltpu.CompilerParams(
            collective_id=0, has_side_effects=True, vmem_limit_bytes=48 * 1024 * 1024
        ),
        cost_estimate=pl.CostEstimate(
            flops=3_000_000_000, bytes_accessed=6_000_000, transcendentals=6_000_000
        ),
    )(*[pltpu.with_memory_space_constraint(a, pltpu.HBM) for a in (hidden, base, down.T, up, decay.T, gain.reshape(HEADS, HD))])
    return mixed, states.reshape(1, HEADS, HD, HD)


def solution(mesh):
    in_specs = (
        P("ctx", "tp"),
        P(None, "ctx", "tp"),
        P("tp", None),
        P(None, None, "tp"),
        P("ctx", "tp"),
        P("tp"),
    )
    out_specs = (P("ctx", "tp"), P("ctx", "tp", None, None))
    return jax.shard_map(local, mesh=mesh, in_specs=in_specs, out_specs=out_specs, check_vma=False)
```

```python
import jax
import jax.numpy as jnp
from jax import lax
from jax.experimental import pallas as pl
from jax.experimental.pallas import tpu as pltpu
from jax.sharding import PartitionSpec as P

HD = 128
HEADS = 4
TOK = 1024
HALF = 512
RANK = 64
GROUP = 384
WIDTH = HEADS * HD
PAIR = 2 * HD
BLK = 256
NX, NY, NZ = 4, 4, 16
NTP = NX * NY
LORA_PIECE = HALF // NTP
CHUNK = HALF // NX
HZ = NZ // 2
OWNERS = 4
LOWER = (2, 3, 4, 5)
UPPER = (13, 12, 10, 9)
EARLY = 7
STATE_PIECE = PAIR // OWNERS
LANES = HD // HEADS
MESH = pl.DeviceIdType.MESH
F32, BF16 = jnp.float32, jnp.bfloat16


def ring(offset, size):
    return min(offset, size - offset)


XY = sorted(range(1, NTP), key=lambda r: -(ring(r // NY, NX) + ring(r % NY, NY)))
ZH = [4, 3, 5, 2, 6, 1, 7]


def order(z):
    return jnp.where(z < HZ, z, jnp.where(z >= 12, 23 - z, z + 4))


CROSS = sorted({*LOWER, *range(EARLY, HZ)})
ORDER = [z if z < HZ else (23 - z if z >= 12 else z + 4) for z in range(NZ)]


def silu(v):
    half = 0.5 * v
    return half + half * jnp.tanh(half)


def kernel(
    hid_hbm, base_hbm, dwn_hbm, up_hbm, dec_hbm, gain_hbm,
    out_v, st_v,
    hid, base, dpad, upad, dec, gain, kbase, kup,
    part, rsum, lora,
    cum, wgt, ccol, dl_own, dl_peer, dl_chip, chip_decay,
    q_ref, qs_ref, kt_ref, v_ref, inside,
    loc, loc_send, loc_recv, tot, p1, pre, later_part, c2, carried,
    in_sem,
    rs_s, rs_r, ag_s, ag_r, zs_s, zs_r, zg_s, zg_r, dz_s, dz_r, core_s, core_r, near_sem, far_sem,
):
    ctx, tp = lax.axis_index("ctx"), lax.axis_index("tp")
    z, c = ctx // 2, ctx % 2
    x, y = tp // NY, tp % NY
    peer = {"ctx": z * 2 + (1 - c)}

    def plane(r):
        return {"tp": lax.rem(x + r // NY, NX) * NY + lax.rem(y + r % NY, NY)}

    zh = z % HZ
    base_z = z - zh
    lower = z < HZ

    def chip(other):
        return {"ctx": other * 2 + c}

    def along(r):
        return base_z + lax.rem(zh + r, HZ)

    loads = [
        pltpu.make_async_copy(dwn_hbm, dpad.at[pl.ds(RANK, RANK)], in_sem.at[0]),
        pltpu.make_async_copy(hid_hbm, hid, in_sem.at[1]),
        pltpu.make_async_copy(dec_hbm, dec, in_sem.at[2]),
        pltpu.make_async_copy(up_hbm, upad.at[:, pl.ds(RANK, RANK)], in_sem.at[3]),
        pltpu.make_async_copy(base_hbm, base, in_sem.at[4]),
        pltpu.make_async_copy(gain_hbm, gain, in_sem.at[5]),
    ]
    loads[0].start()
    loads[1].start()

    place = order(z)
    barrier = pltpu.get_barrier_semaphore()
    for r in XY:
        pl.semaphore_signal(barrier, inc=1, device_id=plane(r), device_id_type=MESH)
    pl.semaphore_signal(barrier, inc=1, device_id=peer, device_id_type=MESH)
    for load in loads[2:]:
        load.start()
    for k in range(NZ):
        @pl.when(place < ORDER[k])
        def _(k=k):
            pl.semaphore_signal(barrier, inc=1, device_id=chip(k), device_id_type=MESH)

    zeros = jnp.zeros((RANK, GROUP), BF16)
    dpad[pl.ds(0, RANK), :] = zeros
    dpad[pl.ds(2 * RANK, RANK), :] = zeros
    zeros = jnp.zeros((RANK, WIDTH), BF16)
    for i in range(3):
        upad[i, pl.ds(0, RANK), :] = zeros
        upad[i, pl.ds(2 * RANK, RANK), :] = zeros

    loads[0].wait()
    loads[1].wait()
    trans_b = (((1,), (1,)), ((), ()))
    for i in range(2):
        rows = pl.ds(i * BLK, BLK)
        mine = lax.dot_general(
            hid[rows, :], dpad[pl.ds(RANK, 2 * RANK), :], trans_b, preferred_element_type=F32
        ) + lax.dot_general(
            hid[pl.ds(HALF + i * BLK, BLK), :], dpad[pl.ds(0, 2 * RANK), :], trans_b,
            preferred_element_type=F32,
        )
        part[rows, :] = mine.astype(BF16)

    pl.semaphore_wait(barrier, NTP - 1 + 1 + place)

    def rs(r):
        to = plane(r)
        return pltpu.make_async_remote_copy(
            part.at[pl.ds(pl.multiple_of(to["tp"] * LORA_PIECE, LORA_PIECE), LORA_PIECE)],
            rsum.at[r], rs_s.at[r], rs_r.at[r], device_id=to, device_id_type=MESH,
        )

    for r in XY:
        rs(r).start()

    for k in range(NZ):
        same = lower if k < HZ else jnp.logical_not(lower)

        @pl.when(jnp.logical_and(place > ORDER[k], same))
        def _(k=k):
            pl.semaphore_signal(near_sem, inc=1, device_id=chip(k), device_id_type=MESH)

        @pl.when(jnp.logical_and(place > ORDER[k], jnp.logical_and(jnp.logical_not(same), k in CROSS)))
        def _(k=k):
            pl.semaphore_signal(far_sem, inc=1, device_id=chip(k), device_id_type=MESH)

    loads[2].wait()
    run = jnp.concatenate([dec[...], jnp.zeros((8 - HEADS, TOK), F32)], axis=0)
    lane = lax.broadcasted_iota(jnp.int32, (8, TOK), 1)
    step = 1
    while step < TOK:
        run = run + jnp.where(lane >= step, pltpu.roll(run, step, 1), 0.0)
        step *= 2
    last = run[:, TOK - 1 :]
    cum[...] = run
    wgt[...] = jnp.exp(last - run)
    dl_own[...] = jnp.broadcast_to(last, (8, HD))
    swap_decay = pltpu.make_async_remote_copy(
        dl_own, dl_peer, core_s.at[0], core_r.at[0], device_id=peer, device_id_type=MESH
    )
    swap_decay.start()

    loads[3].wait()
    loads[4].wait()

    def turn(i, carry):
        at = pl.ds(pl.multiple_of(i * BLK, BLK), BLK)
        kbase[:, at] = base[1, at, :].T
        return carry

    lax.fori_loop(0, TOK // BLK, turn, 0)
    kup[0] = upad[1, pl.ds(RANK, 2 * RANK), :].T
    kup[1] = upad[1, pl.ds(0, 2 * RANK), :].T

    swap_decay.wait()
    head_of_lane = lax.broadcasted_iota(jnp.int32, (8, HD), 1) // LANES
    dl_chip[z] = jnp.sum(
        jnp.where(
            head_of_lane == lax.broadcasted_iota(jnp.int32, (8, HD), 0),
            dl_own[...] + dl_peer[...], 0.0,
        ),
        axis=0, keepdims=True,
    )

    def dz(owner):
        return pltpu.make_async_remote_copy(
            dl_chip.at[z], dl_chip.at[z], dz_s.at[owner], dz_r.at[z],
            device_id=chip(owner), device_id_type=MESH,
        )

    def dz_from(k):
        return pltpu.make_async_remote_copy(
            dl_chip.at[k], dl_chip.at[k], dz_s.at[0], dz_r.at[k],
            device_id=peer, device_id_type=MESH,
        )

    def to_owners(what):
        for k in range(OWNERS):
            owner = jnp.where(lower, LOWER[k], UPPER[k])

            @pl.when(owner != z)
            def _(owner=owner, k=k):
                what(owner, k)

    mine_at = pl.ds(pl.multiple_of(tp * LORA_PIECE, LORA_PIECE), LORA_PIECE)
    for r in XY:
        rs(r).wait_recv()
    total = part[mine_at, :].astype(F32)
    for r in range(1, NTP):
        total = total + rsum[r].astype(F32)
    lora[mine_at, :] = total.astype(BF16)

    def ag(r):
        return pltpu.make_async_remote_copy(
            lora.at[mine_at], lora.at[mine_at], ag_s.at[r], ag_r.at[r],
            device_id=plane(r), device_id_type=MESH,
        )

    for r in XY:
        ag(r).start()
    for r in XY:
        rs(r).wait_send()
    later = jnp.where(lower, HZ, NZ) - 1 - place

    @pl.when(later > 0)
    def _():
        pl.semaphore_wait(near_sem, later)

    adds = jnp.logical_or(zh < HZ - 1, jnp.logical_and(lower, EARLY == HZ))

    @pl.when(adds)
    def _():
        to_owners(lambda owner, k: dz(owner).start())

    loads[5].wait()

    def projected(i, a, row, size, lanes):
        return base[i, pl.ds(a * HALF + row, size), lanes].astype(F32) + jnp.dot(
            lora[pl.ds(row, size), :],
            upad[i, pl.ds(RANK - RANK * a, 2 * RANK), lanes],
            preferred_element_type=F32,
        )

    for n, shift in enumerate((0, 1, 3, 2)):
        for ry in range(NY):
            if shift or ry:
                ag(shift * NY + ry).wait_recv()
        row = pl.multiple_of(lax.rem(x + NX - shift, NX) * CHUNK, CHUNK)
        scaled = []
        for a in range(2):
            at = pl.ds(pl.multiple_of(a * HALF + row, CHUNK), CHUNK)
            k = silu(
                kbase[:, at].astype(F32)
                + lax.dot_general(
                    kup[a], lora[pl.ds(row, CHUNK), :], trans_b, preferred_element_type=F32
                )
            ).astype(BF16)
            kt_ref[:, at] = k
            v_ref[at, :] = projected(2, a, row, CHUNK, slice(None)).astype(BF16)
            scaled.append(
                [
                    (k[h * HD : (h + 1) * HD].astype(F32) * wgt[h : h + 1, at]).astype(BF16)
                    for h in range(HEADS)
                ]
            )
        for h in range(HEADS):
            lanes = slice(h * HD, (h + 1) * HD)
            part_sum = sum(
                jnp.dot(
                    scaled[a][h],
                    v_ref[pl.ds(pl.multiple_of(a * HALF + row, CHUNK), CHUNK), lanes],
                    preferred_element_type=F32,
                )
                for a in range(2)
            )
            if n == 0:
                loc[lanes, :] = part_sum
            else:
                loc[lanes, :] += part_sum

    ours = pl.ds(pl.multiple_of(c * PAIR, PAIR), PAIR)
    theirs = pl.ds(pl.multiple_of((1 - c) * PAIR, PAIR), PAIR)
    even = c == 0

    loc_send[...] = loc[theirs, :].astype(BF16)
    swap_local = pltpu.make_async_remote_copy(
        loc_send, loc_recv, core_s.at[1], core_r.at[1], device_id=peer, device_id_type=MESH
    )
    swap_local.start()
    swap_local.wait_recv()

    def per_row(ref, e):
        return jnp.exp(ref[pl.ds(c * 2 + e, 1), :])

    for e in range(2):
        rows = pl.ds(e * HD, HD)
        own = loc[pl.ds(pl.multiple_of(c * PAIR + e * HD, HD), HD), :]
        other = loc_recv[rows, :].astype(F32)
        odd_decay = jnp.where(even, per_row(dl_peer, e), per_row(dl_own, e))
        tot[rows, :] = (
            jnp.where(even, own, other) * odd_decay + jnp.where(even, other, own)
        ).astype(BF16)

    def zs(owner, k):
        return pltpu.make_async_remote_copy(
            tot.at[pl.ds(k * STATE_PIECE, STATE_PIECE)], p1.at[z], zs_s.at[owner], zs_r.at[z],
            device_id=chip(owner), device_id_type=MESH,
        )

    def zs_from(k):
        return pltpu.make_async_remote_copy(
            tot.at[pl.ds(0, STATE_PIECE)], p1.at[k], zs_s.at[0], zs_r.at[k],
            device_id=peer, device_id_type=MESH,
        )

    @pl.when(adds)
    def _():
        to_owners(lambda owner, k: zs(owner, k).start())

    def first():
        return pltpu.make_async_remote_copy(
            tot, c2, core_s.at[3], core_r.at[3], device_id=chip(1), device_id_type=MESH
        )

    @pl.when(z == 0)
    def _():
        first().start()

    far = jnp.logical_and(lower, z >= EARLY)

    def to_far(what):
        for k in range(OWNERS):
            what(UPPER[k], k)

    @pl.when(far)
    def _():
        pl.semaphore_wait(far_sem, HZ)

        def start(owner, k):
            dz(owner).start()
            zs(owner, k).start()

        to_far(start)

    mine_k, partner, owns = 0, 0, z < 0
    for k in range(OWNERS):
        here = jnp.logical_or(z == LOWER[k], z == UPPER[k])
        mine_k = jnp.where(here, k, mine_k)
        partner = jnp.where(here, UPPER[k], partner)
        owns = jnp.logical_or(owns, here)
    piece_at = pl.ds(pl.multiple_of(mine_k * STATE_PIECE, STATE_PIECE), STATE_PIECE)

    def queries(i, carry):
        for a in range(2):
            row = pl.multiple_of(i * BLK, BLK)
            rows = pl.ds(a * HALF + row, BLK)
            q = silu(projected(0, a, row, BLK, slice(None))).astype(BF16)
            q_ref[rows, :] = q
            for h in range(HEADS):
                grow = jnp.exp(ccol[h, rows, :])
                qs_ref[rows, h * HD : (h + 1) * HD] = (
                    q[:, h * HD : (h + 1) * HD].astype(F32) * grow
                ).astype(BF16)
        return carry

    tri = lax.broadcasted_iota(jnp.int32, (BLK, BLK), 0) >= lax.broadcasted_iota(
        jnp.int32, (BLK, BLK), 1
    )

    def attend(h, carry):
        at = pl.ds(pl.multiple_of(h * HD, HD), HD)
        for b in range(TOK // BLK):
            rows = pl.ds(b * BLK, BLK)
            q = q_ref[rows, at]
            col = ccol[h, rows, :]
            col = jnp.concatenate([col, col], axis=1)
            acc = jnp.zeros((BLK, HD), F32)
            for s in range(b + 1):
                cols = pl.ds(s * BLK, BLK)
                spread = col - cum[pl.ds(h, 1), cols]
                if s == b:
                    spread = jnp.where(tri, spread, -1e30)
                score = jnp.dot(q, kt_ref[at, cols], preferred_element_type=F32)
                weight = (jnp.exp(spread) * score).astype(BF16)
                acc = acc + jnp.dot(weight, v_ref[cols, at], preferred_element_type=F32)
            inside[rows, at] = acc
        return carry

    heads_before = jnp.where(z >= 4, 1, 2)
    def ccol_of(h, carry):
        ccol[h] = jnp.broadcast_to(cum[pl.ds(h, 1), :], (HD, TOK)).T
        return carry

    lax.fori_loop(0, HEADS, ccol_of, 0)
    lax.fori_loop(0, HALF // BLK, queries, 0)
    lax.fori_loop(0, heads_before, attend, 0)

    head_lane = (c * 2 + mine_k // 2) * LANES
    lane_of = lax.broadcasted_iota(jnp.int32, (1, 1, HD), 2)

    def arrive(k):
        @pl.when(z != k)
        def _():
            zs_from(k).wait_recv()

    def decays(first, last):
        for k in range(first, last):
            @pl.when(z != k)
            def _(k=k):
                dz_from(k).wait_recv()

        log = jnp.sum(
            jnp.where(lane_of == head_lane, dl_chip[first:last], 0.0), axis=2, keepdims=True
        )
        chip_decay[first:last] = jnp.broadcast_to(jnp.exp(log), (last - first, 1, HD))

    def advance(state, k):
        return chip_decay[k] * state + p1[k].astype(F32)

    def zg(b):
        return pltpu.make_async_remote_copy(
            pre.at[b % HZ], c2.at[piece_at], zg_s.at[b % HZ], zg_r.at[mine_k],
            device_id=chip(b), device_id_type=MESH,
        )

    def zg_from(k):
        rows = pl.ds(k * STATE_PIECE, STATE_PIECE)
        return pltpu.make_async_remote_copy(
            pre.at[0], c2.at[rows], zg_s.at[0], zg_r.at[k], device_id=peer, device_id_type=MESH
        )

    def give(b):
        @pl.when(z != b)
        def _():
            zg(b).start()

    def given(blocks):
        for b in blocks:
            @pl.when(z != b)
            def _(b=b):
                zg(b).wait_send()

    def early():
        return pltpu.make_async_remote_copy(
            pre.at[EARLY % HZ], p1.at[EARLY - 1], zs_s.at[0], zs_r.at[EARLY - 1],
            device_id=chip(partner), device_id_type=MESH,
        )

    @pl.when(jnp.logical_and(owns, lower))
    def _():
        p1[z] = tot[piece_at, :]
        ends = max(HZ - 1, EARLY)
        decays(0, ends)
        state = jnp.zeros((STATE_PIECE, HD), F32)
        for k in range(ends):
            arrive(k)
            state = advance(state, k)
            pre[(k + 1) % HZ] = state.astype(BF16)
            if k == EARLY - 1:
                @pl.when(jnp.logical_not(far))
                def _():
                    pl.semaphore_wait(far_sem, HZ)

                early().start()
            if 1 < k + 1 < HZ:
                give(k + 1)

    @pl.when(jnp.logical_and(owns, jnp.logical_not(lower)))
    def _():
        p1[z] = tot[piece_at, :]
        decays(EARLY, NZ - 1)
        state = jnp.zeros((STATE_PIECE, HD), F32)
        grow = jnp.ones((1, HD), F32)
        grown = {}
        for k in range(EARLY, NZ - 1):
            arrive(k)
            state = advance(state, k)
            grow = grow * chip_decay[k]
            if k >= HZ - 1:
                later_part[k + 1 - HZ] = state
                grown[k + 1] = grow
        zs_from(EARLY - 1).wait_recv()
        start = p1[EARLY - 1].astype(F32)
        for b in (15, 8, 14, 9, 13, 12, 10, 11):
            pre[b - HZ] = (grown[b] * start + later_part[b - HZ]).astype(BF16)
            give(b)

    @pl.when(owns)
    def _():
        c2[piece_at, :] = pre[zh]

    lax.fori_loop(heads_before, HEADS, attend, 0)
    for r in XY:
        ag(r).wait_send()

    swap_local.wait_send()

    @pl.when(adds)
    def _():
        to_owners(lambda owner, k: dz(owner).wait_send())
        to_owners(lambda owner, k: zs(owner, k).wait_send())

    @pl.when(far)
    def _():
        def sent(owner, k):
            dz(owner).wait_send()
            zs(owner, k).wait_send()

        to_far(sent)

    @pl.when(z == 1)
    def _():
        first().wait_recv()

    @pl.when(z == 0)
    def _():
        first().wait_send()
        c2[...] = jnp.zeros_like(c2)

    def swap_carried(e):
        return pltpu.make_async_remote_copy(
            loc_send.at[pl.ds(e * HD, HD)],
            carried.at[pl.ds(pl.multiple_of(c * PAIR + e * HD, HD), HD)],
            core_s.at[2 + 2 * e], core_r.at[2 + 2 * e], device_id=peer, device_id_type=MESH,
        )

    states = []
    for e in range(2):
        @pl.when(z > 1)
        def _(e=e):
            for k in (2 * e, 2 * e + 1):
                @pl.when(z != jnp.where(lower, LOWER[k], UPPER[k]))
                def _(k=k):
                    zg_from(k).wait_recv()

        rows = pl.ds(e * HD, HD)
        own = loc[pl.ds(pl.multiple_of(c * PAIR + e * HD, HD), HD), :]
        before = c2[rows, :].astype(F32)
        even_decay = jnp.where(even, per_row(dl_own, e), per_row(dl_peer, e))
        after = even_decay * before + jnp.where(even, own, loc_recv[rows, :].astype(F32))
        loc_send[rows, :] = jnp.where(even, after, before).astype(BF16)
        swap_carried(e).start()
        states.append((own, jnp.where(even, before, after)))
    for e, (own, here) in enumerate(states):
        at = pl.ds(pl.multiple_of(c * PAIR + e * HD, HD), HD)
        carried[at, :] = here.astype(BF16)
        st_v[at, :] = per_row(dl_own, e) * here + own

    def finish(i, carry):
        pair = jnp.where(i == 0, c, 1 - c)

        @pl.when(i == 1)
        def _():
            for e in range(2):
                swap_carried(e).wait_recv()
            for e in range(2):
                at = pl.ds(pl.multiple_of((1 - c) * PAIR + e * HD, HD), HD)
                decay = jnp.exp(dl_own[pl.ds((1 - c) * 2 + e, 1), :])
                st_v[at, :] = decay * carried[at, :].astype(F32) + loc[at, :]

        for b in range(TOK // BLK):
            rows = pl.ds(b * BLK, BLK)
            for e in range(2):
                at = pl.ds(pl.multiple_of(pair * PAIR + e * HD, HD), HD)
                att = inside[rows, at] + jnp.dot(
                    qs_ref[rows, at], carried[at, :], preferred_element_type=F32
                )
                square = jnp.mean(att * att, axis=-1, keepdims=True)
                out_v[rows, at] = (
                    att * lax.rsqrt(square + 1e-6) * gain[pl.ds(pair * 2 + e, 1), :]
                ).astype(BF16)
        return carry

    lax.fori_loop(0, 2, finish, 0)
    for e in range(2):
        swap_carried(e).wait_send()

    @pl.when(jnp.logical_and(owns, lower))
    def _():
        given(range(2, HZ))
        early().wait_send()

    @pl.when(jnp.logical_and(owns, jnp.logical_not(lower)))
    def _():
        given(range(HZ, NZ))


def local(hidden, base, down, up, decay, gain):
    anyspace = pl.BlockSpec(memory_space=pl.ANY)
    dma = pltpu.SemaphoreType.DMA
    scratch = [
        pltpu.VMEM((TOK, GROUP), BF16),
        pltpu.VMEM((3, TOK, WIDTH), BF16),
        pltpu.VMEM((3 * RANK, GROUP), BF16),
        pltpu.VMEM((3, 3 * RANK, WIDTH), BF16),
        pltpu.VMEM((HEADS, TOK), F32),
        pltpu.VMEM((HEADS, HD), F32),
        pltpu.VMEM((WIDTH, TOK), BF16),
        pltpu.VMEM((2, WIDTH, 2 * RANK), BF16),
        pltpu.VMEM((HALF, 2 * RANK), BF16),
        pltpu.VMEM((NTP, LORA_PIECE, 2 * RANK), BF16),
        pltpu.VMEM((HALF, 2 * RANK), BF16),
        pltpu.VMEM((8, TOK), F32),
        pltpu.VMEM((8, TOK), F32),
        pltpu.VMEM((HEADS, TOK, HD), F32),
        pltpu.VMEM((8, HD), F32),
        pltpu.VMEM((8, HD), F32),
        pltpu.VMEM((NZ, 1, HD), F32),
        pltpu.VMEM((NZ, 1, HD), F32),
        pltpu.VMEM((TOK, WIDTH), BF16),
        pltpu.VMEM((TOK, WIDTH), BF16),
        pltpu.VMEM((WIDTH, TOK), BF16),
        pltpu.VMEM((TOK, WIDTH), BF16),
        pltpu.VMEM((TOK, WIDTH), F32),
        pltpu.VMEM((WIDTH, HD), F32),
        pltpu.VMEM((PAIR, HD), BF16),
        pltpu.VMEM((PAIR, HD), BF16),
        pltpu.VMEM((PAIR, HD), BF16),
        pltpu.VMEM((NZ, STATE_PIECE, HD), BF16),
        pltpu.VMEM((HZ, STATE_PIECE, HD), BF16),
        pltpu.VMEM((HZ, STATE_PIECE, HD), F32),
        pltpu.VMEM((PAIR, HD), BF16),
        pltpu.VMEM((WIDTH, HD), BF16),
        dma((6,)),
        dma((NTP,)), dma((NTP,)), dma((NTP,)), dma((NTP,)),
        dma((NZ,)), dma((NZ,)), dma((NZ,)), dma((NZ,)), dma((NZ,)), dma((NZ,)),
        dma((5,)), dma((5,)), pltpu.SemaphoreType.REGULAR, pltpu.SemaphoreType.REGULAR,
    ]
    mixed, states = pl.pallas_call(
        kernel,
        out_shape=(
            jax.ShapeDtypeStruct((TOK, WIDTH), BF16),
            jax.ShapeDtypeStruct((WIDTH, HD), F32),
        ),
        in_specs=[anyspace] * 6,
        out_specs=(pl.BlockSpec(memory_space=pltpu.VMEM),) * 2,
        scratch_shapes=scratch,
        compiler_params=pltpu.CompilerParams(
            collective_id=0, has_side_effects=True, vmem_limit_bytes=48 * 1024 * 1024
        ),
        cost_estimate=pl.CostEstimate(
            flops=3_000_000_000, bytes_accessed=6_000_000, transcendentals=6_000_000
        ),
    )(*[pltpu.with_memory_space_constraint(a, pltpu.HBM) for a in (hidden, base, down.T, up, decay.T, gain.reshape(HEADS, HD))])
    return mixed, states.reshape(1, HEADS, HD, HD)


def solution(mesh):
    in_specs = (
        P("ctx", "tp"),
        P(None, "ctx", "tp"),
        P("tp", None),
        P(None, None, "tp"),
        P("ctx", "tp"),
        P("tp"),
    )
    out_specs = (P("ctx", "tp"), P("ctx", "tp", None, None))
    return jax.shard_map(local, mesh=mesh, in_specs=in_specs, out_specs=out_specs, check_vma=False)
```
